256 devices in a mesh: lon: 16 (over y_lo, z), lat: 16 (over y_hi, x, core).
Axes of the slice: x: 4, y: 4 (y_hi: 2, y_lo: 2; y = y_hi * 2 + y_lo), z: 8, core: 2. Of those that a mesh axis runs over, the one named last changes fastest.
Arguments:
- tokens: bfloat16 [768, 288, 512], P('lon', 'lat'), may hold values from -45 to 45
- cotangent: bfloat16 [768, 288, 512], P('lon', 'lat'), may hold values from -6 to 6
- region: int32 [768, 288], P('lon', 'lat'), may hold values from 0 to 2
- gain: float32 [512], replicated, may hold values from 0.25 to 1.75
- w_qkv: bfloat16 [512, 1536], replicated, may hold values from -16 to 16
- w_proj: bfloat16 [512, 512], replicated, may hold values from -0.25 to 0.25
Outputs:
- mixed: bfloat16 [768, 288, 512], P('lon', 'lat')
- tokens_grad: bfloat16 [768, 288, 512], P('lon', 'lat')
- qkv_grad: float32 [512, 1536], replicated
- proj_grad: float32 [512, 512], replicated
- gain_grad: float32 [512], replicated
The draws below stay inside these ranges and needn't reach their ends.
All inputs are finite; a program needn't handle non-finite values.
Results may differ from the reference program's by a relative error of at most 0.011.
Values may be sent and summed in bfloat16 or wider, within the bound.
No kernel may reach another device: no remote copies, remote signals or barrier semaphores. Data moves between devices by JAX's collectives and lax.ppermute only.
A program may use at most 128 MiB of HBM per device.

```python
import jax
import jax.numpy as jnp
from jax import lax

D = 512
HEADS = 8
WIN_LON = 12
WIN_LAT = 6
SHIFT_LON = 6
SHIFT_LAT = 3
LON = 768
LAT = 288


def draw_tokens(key, part):
    key = jax.random.fold_in(key, 11)
    first, second, third = jax.random.split(key, 3)
    base = jnp.clip(jax.random.normal(first, (LON, LAT, D), jnp.float32), -5.0, 5.0)
    row_scales = jnp.exp(jax.random.uniform(second, (LON, LAT, 1), jnp.float32, -1.15, 1.15))
    col_scales = jnp.exp(jax.random.uniform(third, (1, 1, D), jnp.float32, -1.15, 1.15))
    return (base * row_scales * col_scales).astype(jnp.bfloat16)


def draw_w_qkv(key, part):
    key = jax.random.fold_in(key, 23)
    base = jnp.clip(jax.random.normal(key, (D, 3 * D), jnp.float32), -4.0, 4.0) * D ** (-0.5)
    return base.astype(jnp.bfloat16)


def set_ends(drawn, rng, smallest, largest):
    longest = drawn.shape.index(max(drawn.shape))
    spots = []
    for shift in (0, 1):
        where = [jax.random.randint(jax.random.fold_in(rng, axis), (), 0, length) for axis, length in enumerate(drawn.shape)]
        where[longest] = (where[longest] + shift) % drawn.shape[longest]
        spots.append(tuple(where))
    return drawn.at[spots[0]].set(smallest).at[spots[1]].set(largest)


def block_scale(key, shape, shards, least, largest):
    factor_of, own = 1.0, jax.random.fold_in(key, 6)
    for axis_at, parts in shards:
        heights = jnp.exp(jax.random.uniform(jax.random.fold_in(own, axis_at), (parts,), jnp.float32, least / len(shards), largest / len(shards)))
        factor_of = factor_of * jnp.repeat(heights, shape[axis_at] // parts).reshape([-1 if axis == axis_at else 1 for axis in range(len(shape))])
    return factor_of


def scatter_about(rng, dims, spread, bound, cuts=(), kind=jnp.bfloat16):
    array = spread * jax.random.normal(rng, dims, jnp.float32)
    if cuts:
        array = array * block_scale(rng, dims, cuts, -0.22, 0.18)
    return jnp.clip(array, -bound, bound).astype(kind)


def setup_inputs(seed: int = 0) -> dict:
    splits = jax.random.split(jax.random.key(seed), 7)
    return {
        "tokens": draw_tokens(jax.random.fold_in(splits[6], 71), 0),
        "cotangent": scatter_about(splits[1], (LON, LAT, D), 1.0, 6.0, ((0, 16), (1, 16))),
        "region": set_ends(jax.random.randint(splits[2], (LON, LAT), 0, 3), jax.random.fold_in(splits[2], 1), 0, 2).astype(jnp.int32),
        "gain": jnp.clip(1.0 + 0.15 * jax.random.normal(splits[3], (D,), jnp.float32), 0.25, 1.75),
        "w_qkv": draw_w_qkv(jax.random.fold_in(splits[6], 71), 0),
        "w_proj": scatter_about(splits[5], (D, D), D ** -0.5, 0.25),
    }


def to_windows(array_in):
    rows_lon, cols_lat, channels = array_in.shape
    shaped = array_in.reshape(rows_lon // WIN_LON, WIN_LON, cols_lat // WIN_LAT, WIN_LAT, channels)
    return shaped.transpose(0, 2, 1, 3, 4).reshape(-1, WIN_LON * WIN_LAT, channels)

def from_windows(array_in, rows_lon, cols_lat):
    channels = array_in.shape[-1]
    shaped = array_in.reshape(rows_lon // WIN_LON, cols_lat // WIN_LAT, WIN_LON, WIN_LAT, channels)
    return shaped.transpose(0, 2, 1, 3, 4).reshape(rows_lon * cols_lat, channels)

def layer_pass(rolled_x, rolled_g, labels, gain, w_qkv, w_proj):
    rows_lon, cols_lat, channels = rolled_x.shape
    count = rows_lon * cols_lat
    head_dim = channels // HEADS
    score_scale = head_dim ** (-0.5)
    window_len = WIN_LON * WIN_LAT
    flat_input = rolled_x.reshape(count, channels).astype(jnp.float32)
    average = lax.optimization_barrier(jnp.mean(flat_input, axis=-1, keepdims=True))
    centred = flat_input - average
    variance = lax.optimization_barrier(jnp.mean(centred * centred, axis=-1, keepdims=True))
    inverse = lax.rsqrt(variance + 1e-05)
    normed = centred * inverse
    hidden = (normed * gain).astype(jnp.bfloat16)
    projected = jnp.dot(hidden, w_qkv, preferred_element_type=jnp.float32).astype(jnp.bfloat16)
    windowed = to_windows(projected.reshape(rows_lon, cols_lat, 3 * channels))
    windowed = windowed.reshape(-1, window_len, 3, HEADS, head_dim)
    queries = windowed[:, :, 0].astype(jnp.float32)
    keys_win = windowed[:, :, 1].astype(jnp.float32)
    values_win = windowed[:, :, 2].astype(jnp.float32)
    labels_win = to_windows(labels.reshape(rows_lon, cols_lat, 1))[:, :, 0]
    allowed = labels_win[:, :, None] == labels_win[:, None, :]
    scores = jnp.einsum('wihd,wjhd->whij', queries, keys_win) * score_scale
    scores = jnp.where(allowed[:, None], scores, -1e+30)
    row_max = lax.optimization_barrier(jnp.max(scores, axis=-1, keepdims=True))
    lifted = jnp.exp(scores - row_max)
    attention = lifted / lax.optimization_barrier(jnp.sum(lifted, axis=-1, keepdims=True))
    attention_b = attention.astype(jnp.bfloat16)
    attended = jnp.einsum('whij,wjhd->wihd', attention_b.astype(jnp.float32), values_win).astype(jnp.bfloat16)
    attended_flat = from_windows(attended.reshape(-1, window_len, channels), rows_lon, cols_lat)
    branch = jnp.dot(attended_flat, w_proj, preferred_element_type=jnp.float32)
    mixed = (flat_input + branch).astype(jnp.bfloat16)
    upstream = rolled_g.reshape(count, channels)
    grad_proj = jnp.dot(attended_flat.T, upstream, preferred_element_type=jnp.float32)
    grad_attended = jnp.dot(upstream, w_proj.T, preferred_element_type=jnp.float32).astype(jnp.bfloat16)
    grad_att_win = to_windows(grad_attended.reshape(rows_lon, cols_lat, channels))
    grad_att_win = grad_att_win.reshape(-1, window_len, HEADS, head_dim).astype(jnp.float32)
    grad_attention = jnp.einsum('wihd,wjhd->whij', grad_att_win, values_win)
    grad_values = jnp.einsum('whij,wihd->wjhd', attention_b.astype(jnp.float32), grad_att_win)
    inner = lax.optimization_barrier(jnp.sum(grad_attention * attention, axis=-1, keepdims=True))
    grad_scores = (attention * (grad_attention - inner)).astype(jnp.bfloat16).astype(jnp.float32)
    grad_queries = jnp.einsum('whij,wjhd->wihd', grad_scores, keys_win) * score_scale
    grad_keys = jnp.einsum('whij,wihd->wjhd', grad_scores, queries) * score_scale
    grad_stack = jnp.stack([grad_queries, grad_keys, grad_values], 2).astype(jnp.bfloat16)
    grad_projected = from_windows(grad_stack.reshape(-1, window_len, 3 * channels), rows_lon, cols_lat)
    grad_qkv = jnp.dot(hidden.T, grad_projected, preferred_element_type=jnp.float32)
    grad_hidden = jnp.dot(grad_projected, w_qkv.T, preferred_element_type=jnp.float32)
    grad_gain = lax.optimization_barrier(jnp.sum(grad_hidden * normed, axis=0))
    grad_normed = grad_hidden * gain
    grad_input = inverse * (grad_normed - lax.optimization_barrier(jnp.mean(grad_normed, axis=-1, keepdims=True)) - normed * lax.optimization_barrier(jnp.mean(grad_normed * normed, axis=-1, keepdims=True)))
    grad_tokens = (upstream.astype(jnp.float32) + grad_input).astype(jnp.bfloat16)
    return (mixed.reshape(rows_lon, cols_lat, channels), grad_tokens.reshape(rows_lon, cols_lat, channels), grad_qkv, grad_proj, grad_gain)

def reference(tokens, cotangent, region, gain, w_qkv, w_proj):
    channels = tokens.shape[2]
    rolled_x = jnp.roll(tokens, (-SHIFT_LON, -SHIFT_LAT), (0, 1))
    rolled_g = jnp.roll(cotangent, (-SHIFT_LON, -SHIFT_LAT), (0, 1))
    rolled_r = jnp.roll(region, (-SHIFT_LON, -SHIFT_LAT), (0, 1))
    lat_index = jnp.arange(LAT, dtype=jnp.int32)
    wrapped = (lat_index >= LAT - SHIFT_LAT).astype(jnp.int32)
    labels = rolled_r * 2 + wrapped[None, :]
    block_count = LON // WIN_LON

    def visit_block(running, pieces):
        part_x, part_g, part_l = pieces
        mixed, grad_tokens, grad_qkv, grad_proj, grad_gain = layer_pass(part_x, part_g, part_l, gain, w_qkv, w_proj)
        return ((running[0] + grad_qkv, running[1] + grad_proj, running[2] + grad_gain), (mixed, grad_tokens))
    initial = (jnp.zeros((channels, 3 * channels), jnp.float32), jnp.zeros((channels, channels), jnp.float32), jnp.zeros((channels,), jnp.float32))
    totals, outputs = lax.scan(visit_block, initial, (rolled_x.reshape(block_count, WIN_LON, LAT, channels), rolled_g.reshape(block_count, WIN_LON, LAT, channels), labels.reshape(block_count, WIN_LON, LAT)))
    mixed = jnp.roll(outputs[0].reshape(LON, LAT, channels), (SHIFT_LON, SHIFT_LAT), (0, 1))
    grad_tokens = jnp.roll(outputs[1].reshape(LON, LAT, channels), (SHIFT_LON, SHIFT_LAT), (0, 1))
    return (mixed, grad_tokens, totals[0], totals[1], totals[2])
```

```python
import functools

import jax
import jax.numpy as jnp
import numpy as np
from jax import lax
from jax.experimental import pallas as pl
from jax.experimental.pallas import tpu as pltpu
from jax.sharding import Mesh, PartitionSpec as P

HEADS = 8
HEAD_DIM = 64
WIN_LON = 12
WIN_LAT = 6
WIN = WIN_LON * WIN_LAT
SHIFT_LON = 6
SHIFT_LAT = 3
D = 512
ROWS_LON = 48
COLS_LAT = 18
SLAB = WIN_LAT * ROWS_LON
EDGE = 8
HALF = 6 * WIN
F32 = jnp.float32
BF16 = jnp.bfloat16
VMEM_LIMIT = 56 * 1024 * 1024

PLANE = ("y_lo", "y_hi", "x")
LON_AXES = ("y_lo", "z")
LAT_AXES = ("y_hi", "x", "core")


def window_source(window, row):
    jj, ii = divmod(row, WIN_LON)
    return jj, (window * WIN_LON + ii + SHIFT_LON) % ROWS_LON


def inner_pick():
    out = np.zeros((3 * WIN, SLAB), np.float32)
    for window in range(3):
        for row in range(WIN):
            jj, i = window_source(window, row)
            out[window * WIN + row, jj * ROWS_LON + i] = 1
    return out


def edge_pick(column):
    out = np.zeros((WIN, SLAB + COLS_LAT * EDGE), np.float32)
    for row in range(WIN):
        jj, i = window_source(3, row)
        if i >= SHIFT_LON:
            out[row, jj * ROWS_LON + i] = 1
        else:
            out[row, SLAB + (SHIFT_LAT + column * WIN_LAT + jj) * EDGE + i] = 1
    return out


def last_pick():
    third = SHIFT_LAT * ROWS_LON
    out = np.zeros((4 * WIN, 2 * third + COLS_LAT * EDGE + SHIFT_LAT * 2 * EDGE), np.float32)
    for window in range(4):
        for row in range(WIN):
            jj, i = window_source(window, row)
            if i >= SHIFT_LON:
                at = jj * ROWS_LON + i
            elif jj < SHIFT_LAT:
                at = 2 * third + (COLS_LAT - SHIFT_LAT + jj) * EDGE + i
            else:
                at = 2 * third + COLS_LAT * EDGE + (jj - SHIFT_LAT) * 2 * EDGE + i
            out[window * WIN + row, at] = 1
    return out


def slab_place():
    out = np.zeros((SLAB, 4 * WIN), np.float32)
    for window in range(4):
        for row in range(WIN):
            jj, i = window_source(window, row)
            out[jj * ROWS_LON + i, window * WIN + row] = 1
    return out


def dot(a, b):
    return jnp.dot(a, b, preferred_element_type=F32)


def dot_nt(a, b):
    return lax.dot_general(a, b, (((1,), (1,)), ((), ())), preferred_element_type=F32)


def dot_tn(a, b):
    return lax.dot_general(a, b, (((0,), (0,)), ((), ())), preferred_element_type=F32)


def normalise(x):
    centred = x - jnp.mean(x, axis=-1, keepdims=True)
    variance = jnp.mean(centred * centred, axis=-1, keepdims=True)
    inverse = lax.rsqrt(variance + 1e-05)
    return centred * inverse, inverse


def windows_pass(x_w, g_w, lab_w, gain, wqkv, wproj, att_o, dp_o, proj, gatt, onehot, att, dp):
    normed, _ = normalise(x_w[...].astype(F32))
    hidden = (normed * gain[...]).astype(BF16)
    proj[...] = dot(hidden, wqkv[...])
    gatt[...] = dot_nt(g_w[...], wproj[...])
    lane = lax.broadcasted_iota(jnp.int32, (HALF, 128), 1).astype(F32)
    onehot[...] = jnp.where(lab_w == lane, 1.0, 0.0)
    low = lax.broadcasted_iota(jnp.int32, (WIN, 128), 1) < HEAD_DIM

    def stacked(pair):
        return jnp.concatenate([jnp.where(low, pair, 0.0), jnp.where(low, 0.0, pair)], 0)

    def unstacked(both):
        return jnp.where(low, both[:WIN], both[WIN:])

    def one_window(window, _):
        rows = pl.ds(pl.multiple_of(window * WIN, 8), WIN)
        marks = onehot[rows, :]
        marks_q = jnp.concatenate([marks, marks], 0).astype(BF16)
        bar_k = ((marks - 1.0) * 1e30).astype(BF16)
        pairs = range(HEADS // 2)
        q, k, v, do = [], [], [], []
        for pair in pairs:
            cols = pl.ds(pair * 128, 128)
            q.append(stacked(proj[rows, pl.ds(pair * 128, 128)].astype(BF16).astype(F32) * HEAD_DIM**-0.5).astype(BF16))
            k.append(proj[rows, pl.ds(D + pair * 128, 128)].astype(BF16))
            v.append(proj[rows, pl.ds(2 * D + pair * 128, 128)].astype(BF16))
            do.append(stacked(gatt[rows, cols]).astype(BF16))
        s = [dot_nt(jnp.concatenate([k[p], bar_k], 1), jnp.concatenate([q[p], marks_q], 1)) for p in pairs]
        da = [dot_nt(v[p], do[p]) for p in pairs]
        a, ab, ds = [], [], []
        for p in pairs:
            lifted = jnp.exp(s[p] - jnp.max(s[p], axis=0, keepdims=True))
            a.append(lifted * (1.0 / jnp.sum(lifted, axis=0, keepdims=True)))
            ab.append(a[p].astype(BF16))
        for p in pairs:
            inner = jnp.sum(da[p] * a[p], axis=0, keepdims=True)
            ds.append((a[p] * (da[p] - inner)).astype(BF16))
        for p in pairs:
            cols = pl.ds(p * 128, 128)
            att[rows, cols] = unstacked(dot_tn(ab[p], v[p]))
            dp[rows, pl.ds(2 * D + p * 128, 128)] = dot(ab[p], do[p])
            dp[rows, cols] = unstacked(dot_tn(ds[p], k[p])) * HEAD_DIM**-0.5
            dp[rows, pl.ds(D + p * 128, 128)] = dot(ds[p], q[p])
        return 0

    lax.fori_loop(0, 6, one_window, 0)
    att_o[...] = att[...].astype(BF16)
    dp_o[...] = dp[...].astype(BF16)
    return hidden


def first_kernel(x, g, r, pick, gain, wqkv, wproj, x_w, g_w, att_o, dp_o, gqkv, gproj, proj, gatt, onehot, att, dp):
    parts = {}
    for name, ref in (("x", x), ("g", g), ("r", r)):
        got = []
        for column in range(2):
            start = SHIFT_LAT + column * WIN_LAT
            got.append(dot(pick[...], ref[start : start + WIN_LAT].reshape(SLAB, ref.shape[-1])))
        parts[name] = jnp.concatenate(got, 0)
    x_w[...] = parts["x"].astype(BF16)
    g_w[...] = parts["g"].astype(BF16)
    hidden = windows_pass(x_w, g_w, parts["r"], gain, wqkv, wproj, att_o, dp_o, proj, gatt, onehot, att, dp)
    gqkv[...] = dot_tn(hidden, dp_o[...])
    gproj[...] = dot_tn(att_o[...], g_w[...])


def second_kernel(
    where, x, g, r, h_lon, h_lat, h_cor, pick0, pick1, pick2, gain, wqkv, wproj, gqkv1, gproj1,
    x_w, g_w, att_o, dp_o, keep, send, proj, gatt, onehot, att, dp, total,
):
    parts = []
    for first, width, ref in ((0, D, x), (D, D, g), (2 * D, 128, r)):
        lanes = pl.ds(first, width)
        got = []
        for column, pick in ((0, pick0), (1, pick1)):
            start = SHIFT_LAT + column * WIN_LAT
            own = ref[start : start + WIN_LAT].reshape(SLAB, width)
            got.append(dot(pick[...], jnp.concatenate([own, h_lon[:, lanes]], 0)))
        own = ref[COLS_LAT - SHIFT_LAT :].reshape(SHIFT_LAT * ROWS_LON, width)
        got.append(dot(pick2[...], jnp.concatenate([own, h_lat[:, lanes], h_lon[:, lanes], h_cor[:, lanes]], 0)))
        parts.append(jnp.concatenate(got, 0))
    x_w[...] = parts[0].astype(BF16)
    g_w[...] = parts[1].astype(BF16)
    row = lax.broadcasted_iota(jnp.int32, (HALF, 128), 0)
    past = jnp.zeros((HALF, 128), jnp.bool_)
    for window in range(2, 6):
        past = past | ((row >= window * WIN + WIN // 2) & (row < (window + 1) * WIN))
    labels = parts[2] + jnp.where(past, 3.0, 0.0) * where[1].astype(F32)
    hidden = windows_pass(x_w, g_w, labels, gain, wqkv, wproj, att_o, dp_o, proj, gatt, onehot, att, dp)
    total[:, pl.ds(0, 3 * D)] = gqkv1[...] + dot_tn(hidden, dp_o[...])
    total[:, pl.ds(3 * D, D)] = gproj1[...] + dot_tn(att_o[...], g_w[...])
    scaled = jnp.sum(total[:, pl.ds(0, 3 * D)] * wqkv[...].astype(F32), axis=1, keepdims=True)
    diagonal = lax.broadcasted_iota(jnp.int32, (128, 128), 0) == lax.broadcasted_iota(jnp.int32, (128, 128), 1)
    line = [
        jnp.sum(jnp.where(diagonal, scaled[at * 128 : (at + 1) * 128], 0.0), axis=0, keepdims=True) for at in range(4)
    ]
    tile = jnp.concatenate(line + [jnp.zeros((12, 128), F32)], 0).astype(BF16)
    core = where[0]
    for ref, half in ((keep, core), (send, 1 - core)):
        ref[:, pl.ds(0, 4 * D)] = total[pl.ds(pl.multiple_of(half * 256, 256), 256), :].astype(BF16)
        for piece in range(16):
            ref[pl.ds(piece * 16, 16), pl.ds(4 * D, 128)] = tile


def third_kernel(x1, g1, att1, dp1, x2, g2, att2, dp2, place, gain, wqkv, wproj, mixed, tgrad, mixed_f, tgrad_f):
    for at, (x, g, att, dp) in enumerate(((x1, g1, att1, dp1), (x2, g2, att2, dp2))):
        rows = pl.ds(at * HALF, HALF)
        flat = x[...].astype(F32)
        mixed_f[rows, :] = flat + dot(att[...], wproj[...])
        normed, inverse = normalise(flat)
        grad_normed = dot_nt(dp[...], wqkv[...]) * gain[...]
        grad_input = inverse * (
            grad_normed
            - jnp.mean(grad_normed, axis=-1, keepdims=True)
            - normed * jnp.mean(grad_normed * normed, axis=-1, keepdims=True)
        )
        tgrad_f[rows, :] = g[...].astype(F32) + grad_input
    for ref, out in ((mixed_f, mixed), (tgrad_f, tgrad)):
        for column in range(3):
            if column < 2:
                ordered = jnp.concatenate(
                    [ref[pl.ds(column * 3 * WIN, 3 * WIN), :], ref[pl.ds(HALF + column * WIN, WIN), :]], 0
                )
            else:
                ordered = ref[pl.ds(HALF + 2 * WIN, 4 * WIN), :]
            slab = dot(place[...], ordered.astype(BF16)).astype(BF16)
            out[column * WIN_LAT : (column + 1) * WIN_LAT] = slab.reshape(WIN_LAT, ROWS_LON, D)


def pass_scratch():
    return [
        pltpu.VMEM((HALF, 3 * D), F32),
        pltpu.VMEM((HALF, D), F32),
        pltpu.VMEM((HALF, 128), F32),
        pltpu.VMEM((HALF, D), F32),
        pltpu.VMEM((HALF, 3 * D), F32),
    ]


def call(kernel, outs, scratch, flops, name, scalars=0):
    def run(*args):
        specs = [pl.BlockSpec(memory_space=pltpu.SMEM)] * scalars
        specs += [pl.BlockSpec(memory_space=pltpu.VMEM)] * (len(args) - scalars)
        return pl.pallas_call(
            kernel,
            out_shape=[jax.ShapeDtypeStruct(*out) for out in outs],
            in_specs=specs,
            out_specs=[pl.BlockSpec(memory_space=pltpu.VMEM)] * len(outs),
            scratch_shapes=scratch,
            compiler_params=pltpu.CompilerParams(vmem_limit_bytes=VMEM_LIMIT),
            cost_estimate=pl.CostEstimate(flops=flops, bytes_accessed=8 * 2**20, transcendentals=2**19),
            name=name,
        )(*args)

    return run


def swapped(block, axis, size, bit):
    return lax.ppermute(block, axis, [(i, i ^ bit) for i in range(size)])


def reduced(keep, send):
    mine = (keep.astype(F32) + swapped(send, "core", 2, 1).astype(F32)).astype(BF16)
    pieces = lax.all_to_all(mine.reshape(16, 16, -1), PLANE, 0, 0, tiled=True)
    return jnp.sum(pieces.astype(F32), 0).astype(BF16)


def body(tokens, cotangent, region, gain, w_qkv, w_proj):
    x = tokens.transpose(1, 0, 2)
    g = cotangent.transpose(1, 0, 2)
    r = jnp.broadcast_to(region.T.astype(BF16)[:, :, None], (COLS_LAT, ROWS_LON, 128))
    lon_back = [((i + 1) % 16, i) for i in range(16)]
    lat_back = lon_back
    both_back = [(((i + 1) % 16) * 16 + (j + 1) % 16, i * 16 + j) for i in range(16) for j in range(16)]

    def edge(lats, lons):
        return jnp.concatenate([x[lats, lons], g[lats, lons], r[lats, lons]], -1).reshape(-1, 2 * D + 128)

    h_lon = lax.ppermute(edge(slice(None), slice(0, EDGE)), LON_AXES, lon_back)
    h_lat = lax.ppermute(edge(slice(0, SHIFT_LAT), slice(None)), LAT_AXES, lat_back)
    h_cor = lax.ppermute(edge(slice(0, SHIFT_LAT), slice(0, 2 * EDGE)), LON_AXES + LAT_AXES, both_back)

    gain_row = gain.reshape(1, D)
    acts = [((HALF, D), BF16), ((HALF, D), BF16), ((HALF, D), BF16), ((HALF, 3 * D), BF16)]
    constant = functools.partial(jnp.asarray, dtype=BF16)
    x1, g1, att1, dp1, gqkv1, gproj1 = call(
        first_kernel, acts + [((D, 3 * D), F32), ((D, D), F32)], pass_scratch(), 4 * 10**9, "inner"
    )(x, g, r, constant(inner_pick()), gain_row, w_qkv, w_proj)

    where = jnp.stack([lax.axis_index("core"), (lax.axis_index(LAT_AXES) == 15).astype(jnp.int32)]).astype(jnp.int32)
    width = 4 * D + 128
    x2, g2, att2, dp2, keep, send = call(
        second_kernel,
        acts + [((256, width), BF16), ((256, width), BF16)],
        pass_scratch() + [pltpu.VMEM((D, 4 * D), F32)],
        4 * 10**9,
        "outer",
        1,
    )(
        where, x, g, r, h_lon, h_lat, h_cor, constant(edge_pick(0)), constant(edge_pick(1)), constant(last_pick()),
        gain_row, w_qkv, w_proj, gqkv1, gproj1,
    )

    piece = reduced(keep, send)
    piece, x1, x2 = lax.optimization_barrier((piece, x1, x2))
    mixed_c, tgrad_c = call(
        third_kernel,
        [((COLS_LAT, ROWS_LON, D), BF16)] * 2,
        [pltpu.VMEM((2 * HALF, D), F32)] * 2,
        4 * 10**9,
        "tokens",
    )(x1, g1, att1, dp1, x2, g2, att2, dp2, constant(slab_place()), gain_row, w_qkv, w_proj)
    for bit in (1, 2, 4):
        piece = (piece.astype(F32) + swapped(piece, "z", 8, bit).astype(F32)).astype(BF16)

    lon_on = [(j, i) for i, j in lon_back]
    both_on = [(j, i) for i, j in both_back]
    outs = jnp.stack([mixed_c, tgrad_c], 0)
    own = COLS_LAT - SHIFT_LAT
    back_lon = lax.ppermute(outs[:, :own, :EDGE], LON_AXES, lon_on)
    back_lat = lax.ppermute(outs[:, own:], LAT_AXES, lon_on)
    back_cor = lax.ppermute(outs[:, own:, :EDGE], LON_AXES + LAT_AXES, both_on)
    strip = jnp.concatenate([back_cor, back_lon], 1)
    whole = jnp.concatenate([back_lat, outs[:, :own]], 1)
    strip = jnp.pad(strip, ((0, 0), (0, 0), (0, ROWS_LON - EDGE), (0, 0)))
    column = lax.broadcasted_iota(jnp.int32, whole.shape, 2)
    restored = jnp.where(column < SHIFT_LON, strip, whole)
    mixed = restored[0].transpose(1, 0, 2)
    tokens_grad = restored[1].transpose(1, 0, 2)

    gain_grad = piece[:4, 4 * D :].astype(F32).reshape(D) / gain
    grads = lax.all_to_all(jnp.broadcast_to(piece[None, :, : 4 * D], (16, 16, 4 * D)), PLANE, 0, 0, tiled=True)
    grads = grads.reshape(256, 4 * D)
    other = swapped(grads, "core", 2, 1)
    first = lax.axis_index("core") == 0
    full = jnp.concatenate([jnp.where(first, grads, other), jnp.where(first, other, grads)], 0).astype(F32)
    return mixed, tokens_grad, full[:, : 3 * D], full[:, 3 * D :], gain_grad


def solution(mesh):
    fine = Mesh(mesh.devices.reshape(2, 8, 2, 4, 2), ("y_lo", "z", "y_hi", "x", "core"))
    grid = P(LON_AXES, LAT_AXES, None)
    return jax.shard_map(
        body,
        mesh=fine,
        in_specs=(grid, grid, P(LON_AXES, LAT_AXES), P(), P(), P()),
        out_specs=(grid, grid, P(), P(), P()),
        check_vma=False,
    )
```

```python
import functools

import jax
import jax.numpy as jnp
import numpy as np
from jax import lax
from jax.experimental import pallas as pl
from jax.experimental.pallas import tpu as pltpu
from jax.sharding import Mesh, PartitionSpec as P

HEADS = 8
HEAD_DIM = 64
WIN_LON = 12
WIN_LAT = 6
WIN = WIN_LON * WIN_LAT
SHIFT_LON = 6
SHIFT_LAT = 3
D = 512
ROWS_LON = 48
COLS_LAT = 18
SLAB = WIN_LAT * ROWS_LON
EDGE = 8
HALF = 6 * WIN
LON_ROWS, LAT_ROWS, COR_ROWS = 96, 128, 32
LON_IDS, LAT_IDS, COR_IDS = 90, 126, 18
F32 = jnp.float32
BF16 = jnp.bfloat16
MIB = 1024 * 1024

PLANE = ("y_lo", "y_hi", "x")
LON_AXES = ("y_lo", "z")
LAT_AXES = ("y_hi", "x", "core")


def window_source(window, row):
    jj, ii = divmod(row, WIN_LON)
    return jj, (window * WIN_LON + ii + SHIFT_LON) % ROWS_LON


def inner_pick():
    out = np.zeros((3 * WIN, SLAB), np.float32)
    for window in range(3):
        for row in range(WIN):
            jj, i = window_source(window, row)
            out[window * WIN + row, jj * ROWS_LON + i] = 1
    return out


def edge_pick(column):
    out = np.zeros((WIN, WIN_LAT * 16 + LON_ROWS), np.float32)
    for row in range(WIN):
        jj, i = window_source(3, row)
        if i >= SHIFT_LON:
            out[row, jj * 16 + i - 32] = 1
        else:
            out[row, WIN_LAT * 16 + (column * WIN_LAT + jj) * SHIFT_LON + i] = 1
    return out


def last_pick():
    own = SHIFT_LAT * ROWS_LON
    out = np.zeros((4 * WIN, own + LAT_ROWS + LON_ROWS + COR_ROWS), np.float32)
    for window in range(4):
        for row in range(WIN):
            jj, i = window_source(window, row)
            if i >= SHIFT_LON and jj < SHIFT_LAT:
                at = jj * ROWS_LON + i
            elif i >= SHIFT_LON:
                at = own + (jj - SHIFT_LAT) * (ROWS_LON - SHIFT_LON) + i - SHIFT_LON
            elif jj < SHIFT_LAT:
                at = own + LAT_ROWS + (2 * WIN_LAT + jj) * SHIFT_LON + i
            else:
                at = own + LAT_ROWS + LON_ROWS + (jj - SHIFT_LAT) * SHIFT_LON + i
            out[window * WIN + row, at] = 1
    return out


def slab_place():
    out = np.zeros((SLAB, 4 * WIN), np.float32)
    for window in range(4):
        for row in range(WIN):
            jj, i = window_source(window, row)
            out[jj * ROWS_LON + i, window * WIN + row] = 1
    return out


def dot(a, b):
    return jnp.dot(a, b, preferred_element_type=F32)


def dot_nt(a, b):
    return lax.dot_general(a, b, (((1,), (1,)), ((), ())), preferred_element_type=F32)


def dot_tn(a, b):
    return lax.dot_general(a, b, (((0,), (0,)), ((), ())), preferred_element_type=F32)


def normalise(x):
    centred = x - jnp.mean(x, axis=-1, keepdims=True)
    variance = jnp.mean(centred * centred, axis=-1, keepdims=True)
    inverse = lax.rsqrt(variance + 1e-05)
    return centred * inverse, inverse


def staged(pairs, sems):
    copies = [pltpu.make_async_copy(source, scratch, sems.at[at]) for at, (source, scratch) in enumerate(pairs)]
    for copy in copies:
        copy.start()
    return copies


def rows_of(shape, where):
    row = lax.broadcasted_iota(jnp.int32, shape, 0)
    return jnp.where(lax.broadcasted_iota(jnp.int32, shape, 1) == where(row), 1.0, 0.0).astype(BF16)


def strip_row(first, pitch):
    def where(row):
        lat = (row * 10923) >> 16
        return (lat + first) * pitch + row - lat * SHIFT_LON

    return where


def slab_row(row):
    lat = (row >= 42).astype(jnp.int32) + (row >= 84).astype(jnp.int32)
    return jnp.where(row < LAT_IDS, lat * ROWS_LON + SHIFT_LON + row - lat * 42, -1)


def spread_row(kept):
    def where(row):
        lat, lon = row >> 3, row & 7
        return jnp.where((lon < SHIFT_LON) & (lat < kept), lat * SHIFT_LON + lon, -1)

    return where


def wide_row(row):
    lat = (row >= 48).astype(jnp.int32) + (row >= 96).astype(jnp.int32)
    lon = row - lat * ROWS_LON
    return jnp.where(lon >= SHIFT_LON, lat * 42 + lon - SHIFT_LON, -1)


def diagonal(rows):
    shape = (rows, 128)
    return lax.broadcasted_iota(jnp.int32, shape, 0) == lax.broadcasted_iota(jnp.int32, shape, 1)


def region_marks(region, lats):
    columns = region.T
    return jnp.concatenate(
        [jnp.broadcast_to(columns[:, lat : lat + 1], (ROWS_LON, 128)) for lat in lats], 0
    ).astype(BF16)


def windows_pass(x_w, g_w, lab_w, gain, wqkv, wproj, att_b, dp_b, proj, gatt, onehot, att, dp, loads=()):
    normed, _ = normalise(x_w[...].astype(F32))
    hidden = (normed * gain[...]).astype(BF16)
    for load in loads:
        load.wait()
    proj[...] = dot(hidden, wqkv[...])
    gatt[...] = dot_nt(g_w[...], wproj[...])
    lane = lax.broadcasted_iota(jnp.int32, (HALF, 128), 1).astype(F32)
    onehot[...] = jnp.where(lab_w == lane, 1.0, 0.0)
    low = lax.broadcasted_iota(jnp.int32, (WIN, 128), 1) < HEAD_DIM

    def stacked(pair):
        return jnp.concatenate([jnp.where(low, pair, 0.0), jnp.where(low, 0.0, pair)], 0)

    def unstacked(both):
        return jnp.where(low, both[:WIN], both[WIN:])

    def one_window(window):
        rows = pl.ds(window * WIN, WIN)
        marks = onehot[rows, :]
        marks_q = jnp.concatenate([marks, marks], 0).astype(BF16)
        bar_k = ((marks - 1.0) * 1e30).astype(BF16)
        pairs = range(HEADS // 2)
        q, k, v, do = [], [], [], []
        for pair in pairs:
            cols = pl.ds(pair * 128, 128)
            q.append(stacked(proj[rows, pl.ds(pair * 128, 128)].astype(BF16).astype(F32) * HEAD_DIM**-0.5).astype(BF16))
            k.append(proj[rows, pl.ds(D + pair * 128, 128)].astype(BF16))
            v.append(proj[rows, pl.ds(2 * D + pair * 128, 128)].astype(BF16))
            do.append(stacked(gatt[rows, cols]).astype(BF16))
        s = [dot_nt(jnp.concatenate([k[p], bar_k], 1), jnp.concatenate([q[p], marks_q], 1)) for p in pairs]
        da = [dot_nt(v[p], do[p]) for p in pairs]
        a, ab, ds = [], [], []
        for p in pairs:
            lifted = jnp.exp(s[p] - jnp.max(s[p], axis=0, keepdims=True))
            a.append(lifted * (1.0 / jnp.sum(lifted, axis=0, keepdims=True)))
            ab.append(a[p].astype(BF16))
        for p in pairs:
            inner = jnp.sum(da[p] * a[p], axis=0, keepdims=True)
            ds.append((a[p] * (da[p] - inner)).astype(BF16))
        for p in pairs:
            cols = pl.ds(p * 128, 128)
            att[rows, cols] = unstacked(dot_tn(ab[p], v[p]))
            dp[rows, pl.ds(2 * D + p * 128, 128)] = dot(ab[p], do[p])
            dp[rows, cols] = unstacked(dot_tn(ds[p], k[p])) * HEAD_DIM**-0.5
            dp[rows, pl.ds(D + p * 128, 128)] = dot(ds[p], q[p])

    for window in range(6):
        one_window(window)
    att_b[...] = att[...].astype(BF16)
    dp_b[...] = dp[...].astype(BF16)
    return hidden


def first_kernel(
    x_h, g_h, region_h, pick_h, wqkv_h, wproj_h, pick0_h, pick1_h, pick2_h, gain,
    x_o, g_o, att_o, dp_o, gqkv, gproj, wqkv, wproj, pick0, pick1, pick2, strips, tails, region,
    proj, gatt, onehot, att, dp, x_w, g_w, att_b, dp_b, out_sems, x, g, pick, sems,
):
    lats = pl.ds(SHIFT_LAT, 2 * WIN_LAT)
    end = pl.ds(COLS_LAT - SHIFT_LAT, SHIFT_LAT)
    own = [(region_h, region), (pick_h, pick), (x_h.at[lats], x), (g_h.at[lats], g), (wqkv_h, wqkv), (wproj_h, wproj)]
    later = [(pick0_h, pick0), (pick1_h, pick1), (pick2_h, pick2)]
    for at, ref in enumerate((x_h, g_h)):
        later += [(ref.at[lats, pl.ds(32, 16), :], strips.at[at]), (ref.at[end], tails.at[at])]
    loads = staged(own + later, sems)
    for load in loads[:4]:
        load.wait()
    ids = region[...].astype(F32)
    parts = {"r": []}
    for column in range(2):
        start = SHIFT_LAT + column * WIN_LAT
        parts["r"].append(dot(pick[...], region_marks(ids, range(start, start + WIN_LAT))))
    parts["r"] = jnp.concatenate(parts["r"], 0)
    for name, ref in (("x", x), ("g", g)):
        got = []
        for column in range(2):
            start = column * WIN_LAT
            got.append(dot(pick[...], ref[start : start + WIN_LAT].reshape(SLAB, D)))
        parts[name] = jnp.concatenate(got, 0)
    x_w[...] = parts["x"].astype(BF16)
    g_w[...] = parts["g"].astype(BF16)
    stores = staged([(x_w, x_o), (g_w, g_o)], out_sems.at[0])
    hidden = windows_pass(x_w, g_w, parts["r"], gain, wqkv, wproj, att_b, dp_b, proj, gatt, onehot, att, dp, loads[4:6])
    stores += staged([(att_b, att_o), (dp_b, dp_o)], out_sems.at[1])
    gqkv[...] = dot_tn(hidden, dp_b[...])
    gproj[...] = dot_tn(att_b[...], g_w[...])
    for copy in loads[6:] + stores:
        copy.wait()


def second_kernel(
    where, h_lon, h_lat, h_cor, gain, gqkv1, gproj1, wqkv, wproj, pick0, pick1, pick2, strips, tails, region,
    x_o, g_o, att_o, dp_o, keep, send, proj, gatt, onehot, att, dp, x_w, g_w, att_b, dp_b, out_sems, total,
):
    parts = []
    ids = region[...].astype(F32)
    halos = ((h_lon, LON_ROWS, LON_IDS), (h_lat, LAT_ROWS, LAT_IDS), (h_cor, COR_ROWS, COR_IDS))
    for array in range(3):
        if array == 2:
            halo = []
            for packed, rows, at in halos:
                line = packed[pl.ds(at // 16 * 16, 16), pl.ds(0, 128)].astype(F32)[at % 16 : at % 16 + 1]
                column = jnp.sum(jnp.where(diagonal(rows), line, 0.0), axis=1, keepdims=True)
                halo.append(jnp.broadcast_to(column, (rows, 128)).astype(BF16))
        else:
            halo = [packed[:, pl.ds(array * D, D)] for packed, _, _ in halos]

        got = []
        for column, pick in ((0, pick0), (1, pick1)):
            first = column * WIN_LAT
            if array == 2:
                marks = region_marks(ids, range(SHIFT_LAT + first, SHIFT_LAT + first + WIN_LAT))
                own = jnp.concatenate([marks[lat * ROWS_LON + 32 : (lat + 1) * ROWS_LON] for lat in range(WIN_LAT)], 0)
            else:
                own = strips[array, first : first + WIN_LAT].reshape(WIN_LAT * 16, D)
            got.append(dot(pick[...], jnp.concatenate([own, halo[0]], 0)))
        if array == 2:
            own = region_marks(ids, range(COLS_LAT - SHIFT_LAT, COLS_LAT))
        else:
            own = tails[array].reshape(SHIFT_LAT * ROWS_LON, D)
        got.append(dot(pick2[...], jnp.concatenate([own, halo[1], halo[0], halo[2]], 0)))
        parts.append(jnp.concatenate(got, 0))
    x_w[...] = parts[0].astype(BF16)
    g_w[...] = parts[1].astype(BF16)
    stores = staged([(x_w, x_o), (g_w, g_o)], out_sems.at[0])
    row = lax.broadcasted_iota(jnp.int32, (HALF, 128), 0)
    past = jnp.zeros((HALF, 128), jnp.bool_)
    for window in range(2, 6):
        past = past | ((row >= window * WIN + WIN // 2) & (row < (window + 1) * WIN))
    labels = parts[2] + jnp.where(past, 3.0, 0.0) * where[1].astype(F32)
    hidden = windows_pass(x_w, g_w, labels, gain, wqkv, wproj, att_b, dp_b, proj, gatt, onehot, att, dp)
    stores += staged([(att_b, att_o), (dp_b, dp_o)], out_sems.at[1])
    total[:, pl.ds(0, 3 * D)] = gqkv1[...] + dot_tn(hidden, dp_b[...])
    total[:, pl.ds(3 * D, D)] = gproj1[...] + dot_tn(att_b[...], g_w[...])
    scaled = jnp.sum(total[:, pl.ds(0, 3 * D)] * wqkv[...].astype(F32), axis=1, keepdims=True)
    line = [
        jnp.sum(jnp.where(diagonal(128), scaled[at * 128 : (at + 1) * 128], 0.0), axis=0, keepdims=True) for at in range(4)
    ]
    tile = jnp.concatenate(line + [jnp.zeros((12, 128), F32)], 0).astype(BF16)
    core = where[0]
    for ref, half in ((keep, core), (send, 1 - core)):
        ref[:, pl.ds(0, 4 * D)] = total[pl.ds(pl.multiple_of(half * 256, 256), 256), :].astype(BF16)
        for piece in range(16):
            ref[pl.ds(piece * 16, 16), pl.ds(4 * D, 128)] = tile
    for store in stores:
        store.wait()


def third_kernel(
    x1_h, g1_h, att1_h, dp1_h, x2_h, g2_h, att2_h, dp2_h, place_h, wqkv_h, wproj_h, gain,
    mixed, tgrad, s_lon, s_lat, s_cor, mixed_f, tgrad_f, xs, gs, atts, dps, place, wqkv, wproj, sems,
):
    first = [(wproj_h, wproj), (wqkv_h, wqkv), (x1_h, xs.at[0]), (att1_h, atts.at[0]), (dp1_h, dps.at[0])]
    second = [(g1_h, gs.at[0]), (x2_h, xs.at[1]), (att2_h, atts.at[1]), (dp2_h, dps.at[1]), (g2_h, gs.at[1])]
    loads = staged(first + second + [(place_h, place)], sems)
    for at in range(2):
        for load in loads[:6] if at == 0 else loads[6:]:
            load.wait()
        x, g, att, dp = xs.at[at], gs.at[at], atts.at[at], dps.at[at]
        rows = pl.ds(at * HALF, HALF)
        flat = x[...].astype(F32)
        mixed_f[rows, :] = flat + dot(att[...], wproj[...])
        normed, inverse = normalise(flat)
        grad_normed = dot_nt(dp[...], wqkv[...]) * gain[...]
        grad_input = inverse * (
            grad_normed
            - jnp.mean(grad_normed, axis=-1, keepdims=True)
            - normed * jnp.mean(grad_normed * normed, axis=-1, keepdims=True)
        )
        tgrad_f[rows, :] = g[...].astype(F32) + grad_input
    for at, (ref, out) in enumerate(((mixed_f, mixed), (tgrad_f, tgrad))):
        lanes = pl.ds(at * D, D)
        strips = []
        for column in range(3):
            if column < 2:
                ordered = jnp.concatenate(
                    [ref[pl.ds(column * 3 * WIN, 3 * WIN), :], ref[pl.ds(HALF + column * WIN, WIN), :]], 0
                )
            else:
                ordered = ref[pl.ds(HALF + 2 * WIN, 4 * WIN), :]
            slab = dot(place[...], ordered.astype(BF16)).reshape(WIN_LAT, ROWS_LON, D)
            out[column * WIN_LAT : (column + 1) * WIN_LAT] = slab.astype(BF16)
            strips.append(slab[:, :EDGE].reshape(WIN_LAT * EDGE, D))
        strip = jnp.concatenate(strips, 0).astype(BF16)
        last = slab[SHIFT_LAT:].reshape(SHIFT_LAT * ROWS_LON, D).astype(BF16)
        s_lon[:, lanes] = dot(rows_of((LON_ROWS, COLS_LAT * EDGE), strip_row(0, EDGE)), strip).astype(BF16)
        s_lat[:, lanes] = dot(rows_of((LAT_ROWS, SHIFT_LAT * ROWS_LON), slab_row), last).astype(BF16)
        s_cor[:, lanes] = dot(rows_of((COR_ROWS, COLS_LAT * EDGE), strip_row(15, EDGE)), strip).astype(BF16)


def restore_kernel(mixed_c, tgrad_c, h_lon, h_lat, h_cor, mixed, tgrad):
    kept = COLS_LAT - SHIFT_LAT
    first = lax.broadcasted_iota(jnp.int32, (EDGE, D), 0) < SHIFT_LON
    for at, (own, out) in enumerate(((mixed_c, mixed), (tgrad_c, tgrad))):
        lanes = pl.ds(at * D, D)
        out[SHIFT_LAT:] = own[:kept]
        lon = dot(rows_of((kept * EDGE, LON_ROWS), spread_row(kept)), h_lon[:, lanes])
        cor = dot(rows_of((SHIFT_LAT * EDGE, COR_ROWS), spread_row(SHIFT_LAT)), h_cor[:, lanes])
        lat = dot(rows_of((SHIFT_LAT * ROWS_LON, LAT_ROWS), wide_row), h_lat[:, lanes])
        for row in range(COLS_LAT):
            if row < SHIFT_LAT:
                strip = cor[row * EDGE : (row + 1) * EDGE]
                inner = lat[row * ROWS_LON : (row + 1) * ROWS_LON]
                whole = jnp.concatenate([jnp.where(first, strip, inner[:EDGE]), inner[EDGE:]], 0)
                out[row] = whole.astype(BF16)
            else:
                strip = lon[(row - SHIFT_LAT) * EDGE : (row - SHIFT_LAT + 1) * EDGE]
                inner = own[row - SHIFT_LAT, pl.ds(0, 2 * EDGE), :].astype(F32)
                whole = jnp.concatenate([jnp.where(first, strip, inner[:EDGE]), inner[EDGE:]], 0)
                out[row, pl.ds(0, 2 * EDGE), :] = whole.astype(BF16)


def add_kernel(keep, received, out):
    out[...] = (keep[...].astype(F32) + received[...].astype(F32)).astype(BF16)


def sum_kernel(pieces, out):
    total = pieces[0].astype(F32)
    for piece in range(1, 16):
        total = total + pieces[piece].astype(F32)
    out[...] = total.astype(BF16)


def spread_kernel(piece, received, copies, gain):
    total = (piece[...].astype(F32) + received[...].astype(F32)).astype(BF16)
    gain[...] = total[:, 4 * D :].astype(F32)
    for at in range(16):
        copies[at] = total[:, : 4 * D]


def place_kernel(later, half, grads, *refs):
    gqkv, gproj, wide, square, sems = refs[2:] if later else refs
    copies = []
    for part in range(4):
        rows = pl.ds(part * 64, 64)
        wide[rows, :] = grads[rows, pl.ds(0, 3 * D)].astype(F32)
        square[rows, :] = grads[rows, pl.ds(3 * D, D)].astype(F32)
        there = pl.ds(pl.multiple_of(half[0] * 256 + part * 64, 64), 64)
        for at, (source, out) in enumerate(((wide, gqkv), (square, gproj))):
            copies.append(pltpu.make_async_copy(source.at[rows], out.at[there], sems.at[part, at]))
            copies[-1].start()
    for copy in copies:
        copy.wait()


def place(half, grads, *filled):
    hbm = pl.BlockSpec(memory_space=pl.ANY)
    return pl.pallas_call(
        functools.partial(place_kernel, bool(filled)),
        out_shape=[jax.ShapeDtypeStruct((D, 3 * D), F32), jax.ShapeDtypeStruct((D, D), F32)],
        in_specs=[pl.BlockSpec(memory_space=pltpu.SMEM), pl.BlockSpec(memory_space=pltpu.VMEM)] + [hbm] * len(filled),
        out_specs=[hbm, hbm],
        input_output_aliases={2: 0, 3: 1} if filled else {},
        scratch_shapes=[
            pltpu.VMEM((256, 3 * D), F32),
            pltpu.VMEM((256, D), F32),
            pltpu.SemaphoreType.DMA((4, 2)),
        ],
        compiler_params=pltpu.CompilerParams(vmem_limit_bytes=8 * MIB),
        cost_estimate=pl.CostEstimate(flops=10**6, bytes_accessed=3 * 2**20, transcendentals=0),
        name="place",
    )(half, grads, *filled)


def edges_kernel(x_h, g_h, region_h, h_lon, h_lat, h_cor, strips, slabs, region, sems):
    loads = [(region_h, region)]
    for at, ref in enumerate((x_h, g_h)):
        loads += [(ref.at[:, pl.ds(0, 2 * EDGE), :], strips.at[at]), (ref.at[pl.ds(0, SHIFT_LAT)], slabs.at[at])]
    for load in staged(loads, sems):
        load.wait()
    ids = region[...].astype(F32)
    marks = region_marks(ids, range(COLS_LAT))
    strip = jnp.concatenate([marks[lat * ROWS_LON : lat * ROWS_LON + 2 * EDGE] for lat in range(COLS_LAT)], 0)
    width = COLS_LAT * 2 * EDGE
    slab = SHIFT_LAT * ROWS_LON
    for out, rows, at, pick, source in (
        (h_lon, LON_ROWS, LON_IDS, rows_of((LON_ROWS, width), strip_row(SHIFT_LAT, 2 * EDGE)), strip),
        (h_lat, LAT_ROWS, LAT_IDS, rows_of((LAT_ROWS, slab), slab_row), marks[:slab]),
        (h_cor, COR_ROWS, COR_IDS, rows_of((COR_ROWS, width), strip_row(0, 2 * EDGE)), strip),
    ):
        line = jnp.sum(jnp.where(diagonal(rows), dot(pick, source), 0.0), axis=0, keepdims=True)
        line = jnp.concatenate([line] * (D // 128), 1)
        here = lax.broadcasted_iota(jnp.int32, (rows, D), 0) == at
        for array in range(2):
            tokens = slabs[array].reshape(slab, D) if out is h_lat else strips[array].reshape(width, D)
            out[:, pl.ds(array * D, D)] = jnp.where(here, line, dot(pick, tokens)).astype(BF16)


def pass_scratch():
    return [
        pltpu.VMEM((HALF, 3 * D), F32),
        pltpu.VMEM((HALF, D), F32),
        pltpu.VMEM((HALF, 128), F32),
        pltpu.VMEM((HALF, D), F32),
        pltpu.VMEM((HALF, 3 * D), F32),
        pltpu.VMEM((HALF, D), BF16),
        pltpu.VMEM((HALF, D), BF16),
        pltpu.VMEM((HALF, D), BF16),
        pltpu.VMEM((HALF, 3 * D), BF16),
        pltpu.SemaphoreType.DMA((2, 2)),
    ]


def call(kernel, outs, scratch, flops, name, scalars=0, far=0, kept=0, vmem=24):
    def run(*args):
        args = list(args)
        for at in range(scalars, scalars + far):
            args[at] = pltpu.with_memory_space_constraint(args[at], pltpu.HBM)
        specs = [pl.BlockSpec(memory_space=pltpu.SMEM)] * scalars
        specs += [pl.BlockSpec(memory_space=pltpu.HBM)] * far
        specs += [pl.BlockSpec(memory_space=pltpu.VMEM)] * (len(args) - scalars - far)
        return pl.pallas_call(
            kernel,
            out_shape=[pltpu.HBM(*out) if at < kept else jax.ShapeDtypeStruct(*out) for at, out in enumerate(outs)],
            in_specs=specs,
            out_specs=[pl.BlockSpec(memory_space=pltpu.HBM if at < kept else pltpu.VMEM) for at in range(len(outs))],
            scratch_shapes=scratch,
            compiler_params=pltpu.CompilerParams(vmem_limit_bytes=vmem * MIB),
            cost_estimate=pl.CostEstimate(flops=flops, bytes_accessed=8 * 2**20, transcendentals=2**19),
            name=name,
        )(*args)

    return run


def swapped(block, axis, size, bit):
    return lax.ppermute(block, axis, [(i, i ^ bit) for i in range(size)])


def body(tokens, cotangent, region, gain, w_qkv, w_proj):
    x = tokens.transpose(1, 0, 2)
    g = cotangent.transpose(1, 0, 2)
    edges = [((rows, 2 * D), BF16) for rows in (LON_ROWS, LAT_ROWS, COR_ROWS)]
    ids = region.T
    scratch = [pltpu.VMEM((2, COLS_LAT, 2 * EDGE, D), BF16), pltpu.VMEM((2, SHIFT_LAT, ROWS_LON, D), BF16)]
    scratch += [pltpu.VMEM((COLS_LAT, ROWS_LON), jnp.int32), pltpu.SemaphoreType.DMA((5,))]
    e_lon, e_lat, e_cor = call(edges_kernel, edges, scratch, 10**6, "edges", far=3, vmem=8)(x, g, ids)
    lon_back = [((i + 1) % 16, i) for i in range(16)]
    lat_back = lon_back
    both_back = [(((i + 1) % 16) * 16 + (j + 1) % 16, i * 16 + j) for i in range(16) for j in range(16)]

    h_lon = lax.ppermute(e_lon, LON_AXES, lon_back)
    h_lat = lax.ppermute(e_lat, LAT_AXES, lat_back)
    h_cor = lax.ppermute(e_cor, LON_AXES + LAT_AXES, both_back)

    gain_row = gain.reshape(1, D)
    acts = [((HALF, D), BF16), ((HALF, D), BF16), ((HALF, D), BF16), ((HALF, 3 * D), BF16)]
    constant = functools.partial(jnp.asarray, dtype=BF16)
    weights = [((D, 3 * D), BF16), ((D, D), BF16)]
    picks = [inner_pick(), edge_pick(0), edge_pick(1), last_pick()]
    passed = [((D, 3 * D), F32), ((D, D), F32)] + weights + [(pick.shape, BF16) for pick in picks[1:]]
    passed += [((2, 2 * WIN_LAT, 16, D), BF16), ((2, SHIFT_LAT, ROWS_LON, D), BF16), ((COLS_LAT, ROWS_LON), jnp.int32)]
    slabs = [pltpu.VMEM((2 * WIN_LAT, ROWS_LON, D), BF16)] * 2 + [pltpu.VMEM((3 * WIN, SLAB), BF16)]
    picks = [constant(pick) for pick in picks]
    x1, g1, att1, dp1, *passed = call(
        first_kernel,
        acts + passed,
        pass_scratch() + slabs + [pltpu.SemaphoreType.DMA((13,))],
        4 * 10**9,
        "inner",
        far=9,
        kept=4,
    )(x, g, ids, picks[0], w_qkv, w_proj, *picks[1:], gain_row)

    where = jnp.stack([lax.axis_index("core"), (lax.axis_index(LAT_AXES) == 15).astype(jnp.int32)]).astype(jnp.int32)
    width = 4 * D + 128
    x2, g2, att2, dp2, keep, send = call(
        second_kernel,
        acts + [((256, width), BF16), ((256, width), BF16)],
        pass_scratch() + [pltpu.VMEM((D, 4 * D), F32)],
        4 * 10**9,
        "outer",
        1,
        kept=4,
    )(where, h_lon, h_lat, h_cor, gain_row, *passed)

    (mine,) = call(add_kernel, [((256, width), BF16)], [], 10**5, "add", vmem=8)(keep, swapped(send, "core", 2, 1))
    mine, x1, x2 = lax.optimization_barrier((mine, x1, x2))
    pieces = lax.all_to_all(mine.reshape(16, 16, -1), PLANE, 0, 0, tiled=True)
    mixed_c, tgrad_c, s_lon, s_lat, s_cor = call(
        third_kernel,
        [((COLS_LAT, ROWS_LON, D), BF16)] * 2
        + edges,
        [pltpu.VMEM((2 * HALF, D), F32)] * 2
        + [pltpu.VMEM((2, HALF, D), BF16)] * 3
        + [pltpu.VMEM((2, HALF, 3 * D), BF16), pltpu.VMEM((SLAB, 4 * WIN), BF16)]
        + [pltpu.VMEM(*weight) for weight in weights]
        + [pltpu.SemaphoreType.DMA((11,))],
        4 * 10**9,
        "tokens",
        far=11,
        vmem=28,
    )(x1, g1, att1, dp1, x2, g2, att2, dp2, constant(slab_place()), w_qkv, w_proj, gain_row)
    lon_on = [(j, i) for i, j in lon_back]
    both_on = [(j, i) for i, j in both_back]
    t_lon = lax.ppermute(s_lon, LON_AXES, lon_on)
    t_lat = lax.ppermute(s_lat, LAT_AXES, lon_on)
    t_cor = lax.ppermute(s_cor, LON_AXES + LAT_AXES, both_on)

    pieces, t_lon, t_lat, t_cor = lax.optimization_barrier((pieces, t_lon, t_lat, t_cor))
    (piece,) = call(sum_kernel, [((16, width), BF16)], [], 10**5, "sum", vmem=8)(pieces)
    for bit in (1, 2):
        (piece,) = call(add_kernel, [((16, width), BF16)], [], 10**5, "add", vmem=4)(piece, swapped(piece, "z", 8, bit))
    copies, gain_tile = call(spread_kernel, [((16, 16, 4 * D), BF16), ((16, 128), F32)], [], 10**5, "spread", vmem=8)(
        piece, swapped(piece, "z", 8, 6)
    )
    gain_grad = gain_tile[:4].reshape(D) / gain
    grads = lax.all_to_all(copies, PLANE, 0, 0, tiled=True)
    mixed, tokens_grad = call(restore_kernel, [((COLS_LAT, ROWS_LON, D), BF16)] * 2, [], 10**6, "restore", vmem=10)(
        mixed_c, tgrad_c, t_lon, t_lat, t_cor
    )
    grads, mixed, tokens_grad = lax.optimization_barrier((grads, mixed, tokens_grad))
    grads = grads.reshape(256, 4 * D)
    other = swapped(grads, "core", 2, 1)
    core = where[:1]
    qkv_grad, proj_grad = place(1 - core, other, *place(core, grads))

    return mixed.transpose(1, 0, 2), tokens_grad.transpose(1, 0, 2), qkv_grad, proj_grad, gain_grad


def solution(mesh):
    fine = Mesh(mesh.devices.reshape(2, 8, 2, 4, 2), ("y_lo", "z", "y_hi", "x", "core"))
    grid = P(LON_AXES, LAT_AXES, None)
    return jax.shard_map(
        body,
        mesh=fine,
        in_specs=(grid, grid, P(LON_AXES, LAT_AXES), P(), P(), P()),
        out_specs=(grid, grid, P(), P(), P()),
        check_vma=False,
    )
```

```python
import functools

import jax
import jax.numpy as jnp
import numpy as np
from jax import lax
from jax.experimental import pallas as pl
from jax.experimental.pallas import tpu as pltpu
from jax.sharding import Mesh, PartitionSpec as P

HEADS = 8
HEAD_DIM = 64
WIN_LON = 12
WIN_LAT = 6
WIN = WIN_LON * WIN_LAT
SHIFT_LON = 6
SHIFT_LAT = 3
D = 512
ROWS_LON = 48
COLS_LAT = 18
SLAB = WIN_LAT * ROWS_LON
EDGE = 8
HALF = 6 * WIN
LON_ROWS, LAT_ROWS, COR_ROWS = 96, 128, 32
LON_IDS, LAT_IDS, COR_IDS = 90, 126, 18
F32 = jnp.float32
BF16 = jnp.bfloat16
MIB = 1024 * 1024

PLANE = ("y_lo", "y_hi", "x")
LON_AXES = ("y_lo", "z")
LAT_AXES = ("y_hi", "x", "core")


def window_source(window, row):
    jj, ii = divmod(row, WIN_LON)
    return jj, (window * WIN_LON + ii + SHIFT_LON) % ROWS_LON


def inner_pick():
    out = np.zeros((3 * WIN, SLAB), np.float32)
    for window in range(3):
        for row in range(WIN):
            jj, i = window_source(window, row)
            out[window * WIN + row, jj * ROWS_LON + i] = 1
    return out


def edge_pick(column):
    out = np.zeros((WIN, WIN_LAT * 16 + LON_ROWS), np.float32)
    for row in range(WIN):
        jj, i = window_source(3, row)
        if i >= SHIFT_LON:
            out[row, jj * 16 + i - 32] = 1
        else:
            out[row, WIN_LAT * 16 + (column * WIN_LAT + jj) * SHIFT_LON + i] = 1
    return out


def last_pick():
    own = SHIFT_LAT * ROWS_LON
    out = np.zeros((4 * WIN, own + LAT_ROWS + LON_ROWS + COR_ROWS), np.float32)
    for window in range(4):
        for row in range(WIN):
            jj, i = window_source(window, row)
            if i >= SHIFT_LON and jj < SHIFT_LAT:
                at = jj * ROWS_LON + i
            elif i >= SHIFT_LON:
                at = own + (jj - SHIFT_LAT) * (ROWS_LON - SHIFT_LON) + i - SHIFT_LON
            elif jj < SHIFT_LAT:
                at = own + LAT_ROWS + (2 * WIN_LAT + jj) * SHIFT_LON + i
            else:
                at = own + LAT_ROWS + LON_ROWS + (jj - SHIFT_LAT) * SHIFT_LON + i
            out[window * WIN + row, at] = 1
    return out


def slab_place():
    out = np.zeros((SLAB, 4 * WIN), np.float32)
    for window in range(4):
        for row in range(WIN):
            jj, i = window_source(window, row)
            out[jj * ROWS_LON + i, window * WIN + row] = 1
    return out


def dot(a, b):
    return jnp.dot(a, b, preferred_element_type=F32)


def dot_nt(a, b):
    return lax.dot_general(a, b, (((1,), (1,)), ((), ())), preferred_element_type=F32)


def dot_tn(a, b):
    return lax.dot_general(a, b, (((0,), (0,)), ((), ())), preferred_element_type=F32)


def normalise(x):
    centred = x - jnp.mean(x, axis=-1, keepdims=True)
    variance = jnp.mean(centred * centred, axis=-1, keepdims=True)
    inverse = lax.rsqrt(variance + 1e-05)
    return centred * inverse, inverse


def staged(pairs, sems):
    copies = [pltpu.make_async_copy(source, scratch, sems.at[at]) for at, (source, scratch) in enumerate(pairs)]
    for copy in copies:
        copy.start()
    return copies


def rows_of(shape, where):
    row = lax.broadcasted_iota(jnp.int32, shape, 0)
    return jnp.where(lax.broadcasted_iota(jnp.int32, shape, 1) == where(row), 1.0, 0.0).astype(BF16)


def strip_row(first, pitch):
    def where(row):
        lat = (row * 10923) >> 16
        return (lat + first) * pitch + row - lat * SHIFT_LON

    return where


def slab_row(row):
    lat = (row >= 42).astype(jnp.int32) + (row >= 84).astype(jnp.int32)
    return jnp.where(row < LAT_IDS, lat * ROWS_LON + SHIFT_LON + row - lat * 42, -1)


def spread_row(kept):
    def where(row):
        lat, lon = row >> 3, row & 7
        return jnp.where((lon < SHIFT_LON) & (lat < kept), lat * SHIFT_LON + lon, -1)

    return where


def wide_row(row):
    lat = (row >= 48).astype(jnp.int32) + (row >= 96).astype(jnp.int32)
    lon = row - lat * ROWS_LON
    return jnp.where(lon >= SHIFT_LON, lat * 42 + lon - SHIFT_LON, -1)


def diagonal(rows):
    shape = (rows, 128)
    return lax.broadcasted_iota(jnp.int32, shape, 0) == lax.broadcasted_iota(jnp.int32, shape, 1)


def region_marks(region, lats):
    columns = region.T
    return jnp.concatenate(
        [jnp.broadcast_to(columns[:, lat : lat + 1], (ROWS_LON, 128)) for lat in lats], 0
    ).astype(BF16)


def windows_pass(x_w, g_w, lab_w, gain, wqkv, wproj, att_b, dp_b, proj, gatt, onehot, att, dp, loads=()):
    normed, _ = normalise(x_w[...].astype(F32))
    hidden = (normed * gain[...]).astype(BF16)
    for load in loads:
        load.wait()
    proj[...] = dot(hidden, wqkv[...])
    gatt[...] = dot_nt(g_w[...], wproj[...])
    lane = lax.broadcasted_iota(jnp.int32, (HALF, 128), 1).astype(F32)
    onehot[...] = jnp.where(lab_w == lane, 1.0, 0.0)
    low = lax.broadcasted_iota(jnp.int32, (WIN, 128), 1) < HEAD_DIM

    def stacked(pair):
        return jnp.concatenate([jnp.where(low, pair, 0.0), jnp.where(low, 0.0, pair)], 0)

    def unstacked(both):
        return jnp.where(low, both[:WIN], both[WIN:])

    def one_window(window):
        rows = pl.ds(window * WIN, WIN)
        marks = onehot[rows, :]
        marks_q = jnp.concatenate([marks, marks], 0).astype(BF16)
        bar_k = ((marks - 1.0) * 1e30).astype(BF16)
        pairs = range(HEADS // 2)
        q, k, v, do = [], [], [], []
        for pair in pairs:
            cols = pl.ds(pair * 128, 128)
            q.append(stacked(proj[rows, pl.ds(pair * 128, 128)].astype(BF16).astype(F32) * HEAD_DIM**-0.5).astype(BF16))
            k.append(proj[rows, pl.ds(D + pair * 128, 128)].astype(BF16))
            v.append(proj[rows, pl.ds(2 * D + pair * 128, 128)].astype(BF16))
            do.append(stacked(gatt[rows, cols]).astype(BF16))
        s = [dot_nt(jnp.concatenate([k[p], bar_k], 1), jnp.concatenate([q[p], marks_q], 1)) for p in pairs]
        da = [dot_nt(v[p], do[p]) for p in pairs]
        a, ab, ds = [], [], []
        for p in pairs:
            lifted = jnp.exp(s[p] - jnp.max(s[p], axis=0, keepdims=True))
            a.append(lifted * (1.0 / jnp.sum(lifted, axis=0, keepdims=True)))
            ab.append(a[p].astype(BF16))
        for p in pairs:
            inner = jnp.sum(da[p] * a[p], axis=0, keepdims=True)
            ds.append((a[p] * (da[p] - inner)).astype(BF16))
        for p in pairs:
            cols = pl.ds(p * 128, 128)
            att[rows, cols] = unstacked(dot_tn(ab[p], v[p]))
            dp[rows, pl.ds(2 * D + p * 128, 128)] = dot(ab[p], do[p])
            dp[rows, cols] = unstacked(dot_tn(ds[p], k[p])) * HEAD_DIM**-0.5
            dp[rows, pl.ds(D + p * 128, 128)] = dot(ds[p], q[p])

    for window in range(6):
        one_window(window)
    att_b[...] = att[...].astype(BF16)
    dp_b[...] = dp[...].astype(BF16)
    return hidden


def first_kernel(
    x_h, g_h, region_h, pick_h, wqkv_h, wproj_h, pick0_h, pick1_h, pick2_h, gain,
    x_o, g_o, att_o, dp_o, gqkv, gproj, wqkv, wproj, pick0, pick1, pick2, strips, tails, region,
    proj, gatt, onehot, att, dp, x_w, g_w, att_b, dp_b, out_sems, x, g, pick, sems,
):
    lats = pl.ds(SHIFT_LAT, 2 * WIN_LAT)
    end = pl.ds(COLS_LAT - SHIFT_LAT, SHIFT_LAT)
    own = [(region_h, region), (pick_h, pick), (x_h.at[lats], x), (g_h.at[lats], g), (wqkv_h, wqkv), (wproj_h, wproj)]
    later = [(pick0_h, pick0), (pick1_h, pick1), (pick2_h, pick2)]
    for at, ref in enumerate((x_h, g_h)):
        later += [(ref.at[lats, pl.ds(32, 16), :], strips.at[at]), (ref.at[end], tails.at[at])]
    loads = staged(own + later, sems)
    for load in loads[:4]:
        load.wait()
    ids = region[...].astype(F32)
    parts = {"r": []}
    for column in range(2):
        start = SHIFT_LAT + column * WIN_LAT
        parts["r"].append(dot(pick[...], region_marks(ids, range(start, start + WIN_LAT))))
    parts["r"] = jnp.concatenate(parts["r"], 0)
    for name, ref in (("x", x), ("g", g)):
        got = []
        for column in range(2):
            start = column * WIN_LAT
            got.append(dot(pick[...], ref[start : start + WIN_LAT].reshape(SLAB, D)))
        parts[name] = jnp.concatenate(got, 0)
    x_w[...] = parts["x"].astype(BF16)
    g_w[...] = parts["g"].astype(BF16)
    stores = staged([(x_w, x_o), (g_w, g_o)], out_sems.at[0])
    hidden = windows_pass(x_w, g_w, parts["r"], gain, wqkv, wproj, att_b, dp_b, proj, gatt, onehot, att, dp, loads[4:6])
    stores += staged([(att_b, att_o), (dp_b, dp_o)], out_sems.at[1])
    gqkv[...] = dot_tn(hidden, dp_b[...])
    gproj[...] = dot_tn(att_b[...], g_w[...])
    for copy in loads[6:] + stores:
        copy.wait()


def second_kernel(
    where, h_lon, h_lat, h_cor, gain, gqkv1, gproj1, wqkv, wproj, pick0, pick1, pick2, strips, tails, region,
    x_o, g_o, att_o, dp_o, keep, send, proj, gatt, onehot, att, dp, x_w, g_w, att_b, dp_b, out_sems, total,
):
    parts = []
    ids = region[...].astype(F32)
    halos = ((h_lon, LON_ROWS, LON_IDS), (h_lat, LAT_ROWS, LAT_IDS), (h_cor, COR_ROWS, COR_IDS))
    for array in range(3):
        if array == 2:
            halo = []
            for packed, rows, at in halos:
                line = packed[pl.ds(at // 16 * 16, 16), pl.ds(0, 128)].astype(F32)[at % 16 : at % 16 + 1]
                column = jnp.sum(jnp.where(diagonal(rows), line, 0.0), axis=1, keepdims=True)
                halo.append(jnp.broadcast_to(column, (rows, 128)).astype(BF16))
        else:
            halo = [packed[:, pl.ds(array * D, D)] for packed, _, _ in halos]

        got = []
        for column, pick in ((0, pick0), (1, pick1)):
            first = column * WIN_LAT
            if array == 2:
                marks = region_marks(ids, range(SHIFT_LAT + first, SHIFT_LAT + first + WIN_LAT))
                own = jnp.concatenate([marks[lat * ROWS_LON + 32 : (lat + 1) * ROWS_LON] for lat in range(WIN_LAT)], 0)
            else:
                own = strips[array, first : first + WIN_LAT].reshape(WIN_LAT * 16, D)
            got.append(dot(pick[...], jnp.concatenate([own, halo[0]], 0)))
        if array == 2:
            own = region_marks(ids, range(COLS_LAT - SHIFT_LAT, COLS_LAT))
        else:
            own = tails[array].reshape(SHIFT_LAT * ROWS_LON, D)
        got.append(dot(pick2[...], jnp.concatenate([own, halo[1], halo[0], halo[2]], 0)))
        parts.append(jnp.concatenate(got, 0))
    x_w[...] = parts[0].astype(BF16)
    g_w[...] = parts[1].astype(BF16)
    stores = staged([(x_w, x_o), (g_w, g_o)], out_sems.at[0])
    row = lax.broadcasted_iota(jnp.int32, (HALF, 128), 0)
    past = jnp.zeros((HALF, 128), jnp.bool_)
    for window in range(2, 6):
        past = past | ((row >= window * WIN + WIN // 2) & (row < (window + 1) * WIN))
    labels = parts[2] + jnp.where(past, 3.0, 0.0) * where[1].astype(F32)
    hidden = windows_pass(x_w, g_w, labels, gain, wqkv, wproj, att_b, dp_b, proj, gatt, onehot, att, dp)
    stores += staged([(att_b, att_o), (dp_b, dp_o)], out_sems.at[1])
    total[:, pl.ds(0, 3 * D)] = gqkv1[...] + dot_tn(hidden, dp_b[...])
    total[:, pl.ds(3 * D, D)] = gproj1[...] + dot_tn(att_b[...], g_w[...])
    scaled = jnp.sum(total[:, pl.ds(0, 3 * D)] * wqkv[...].astype(F32), axis=1, keepdims=True)
    line = [
        jnp.sum(jnp.where(diagonal(128), scaled[at * 128 : (at + 1) * 128], 0.0), axis=0, keepdims=True) for at in range(4)
    ]
    tile = jnp.concatenate(line + [jnp.zeros((12, 128), F32)], 0).astype(BF16)
    core = where[0]
    for ref, half in ((keep, core), (send, 1 - core)):
        ref[:, pl.ds(0, 4 * D)] = total[pl.ds(pl.multiple_of(half * 256, 256), 256), :].astype(BF16)
        for piece in range(16):
            ref[pl.ds(piece * 16, 16), pl.ds(4 * D, 128)] = tile
    for store in stores:
        store.wait()


def third_kernel(
    x1_h, g1_h, att1_h, dp1_h, x2_h, g2_h, att2_h, dp2_h, place_h, wqkv_h, wproj_h, gain,
    mixed, tgrad, s_lon, s_lat, s_cor, mixed_f, tgrad_f, xs, gs, atts, dps, place, wqkv, wproj, sems,
):
    first = [(wproj_h, wproj), (wqkv_h, wqkv), (x1_h, xs.at[0]), (att1_h, atts.at[0]), (dp1_h, dps.at[0])]
    second = [(g1_h, gs.at[0]), (x2_h, xs.at[1]), (att2_h, atts.at[1]), (dp2_h, dps.at[1]), (g2_h, gs.at[1])]
    loads = staged(first + second + [(place_h, place)], sems)
    for at in range(2):
        for load in loads[:6] if at == 0 else loads[6:]:
            load.wait()
        x, g, att, dp = xs.at[at], gs.at[at], atts.at[at], dps.at[at]
        rows = pl.ds(at * HALF, HALF)
        flat = x[...].astype(F32)
        mixed_f[rows, :] = flat + dot(att[...], wproj[...])
        normed, inverse = normalise(flat)
        grad_normed = dot_nt(dp[...], wqkv[...]) * gain[...]
        grad_input = inverse * (
            grad_normed
            - jnp.mean(grad_normed, axis=-1, keepdims=True)
            - normed * jnp.mean(grad_normed * normed, axis=-1, keepdims=True)
        )
        tgrad_f[rows, :] = g[...].astype(F32) + grad_input
    for at, (ref, out) in enumerate(((mixed_f, mixed), (tgrad_f, tgrad))):
        lanes = pl.ds(at * D, D)
        strips = []
        for column in range(3):
            if column < 2:
                ordered = jnp.concatenate(
                    [ref[pl.ds(column * 3 * WIN, 3 * WIN), :], ref[pl.ds(HALF + column * WIN, WIN), :]], 0
                )
            else:
                ordered = ref[pl.ds(HALF + 2 * WIN, 4 * WIN), :]
            slab = dot(place[...], ordered.astype(BF16)).reshape(WIN_LAT, ROWS_LON, D)
            out[column * WIN_LAT : (column + 1) * WIN_LAT] = slab.astype(BF16)
            strips.append(slab[:, :EDGE].reshape(WIN_LAT * EDGE, D))
        strip = jnp.concatenate(strips, 0).astype(BF16)
        last = slab[SHIFT_LAT:].reshape(SHIFT_LAT * ROWS_LON, D).astype(BF16)
        s_lon[:, lanes] = dot(rows_of((LON_ROWS, COLS_LAT * EDGE), strip_row(0, EDGE)), strip).astype(BF16)
        s_lat[:, lanes] = dot(rows_of((LAT_ROWS, SHIFT_LAT * ROWS_LON), slab_row), last).astype(BF16)
        s_cor[:, lanes] = dot(rows_of((COR_ROWS, COLS_LAT * EDGE), strip_row(15, EDGE)), strip).astype(BF16)


def restore_kernel(mixed_c, tgrad_c, h_lon, h_lat, h_cor, mixed, tgrad):
    kept = COLS_LAT - SHIFT_LAT
    first = lax.broadcasted_iota(jnp.int32, (EDGE, D), 0) < SHIFT_LON
    for at, (own, out) in enumerate(((mixed_c, mixed), (tgrad_c, tgrad))):
        lanes = pl.ds(at * D, D)
        out[SHIFT_LAT:] = own[:kept]
        lon = dot(rows_of((kept * EDGE, LON_ROWS), spread_row(kept)), h_lon[:, lanes])
        cor = dot(rows_of((SHIFT_LAT * EDGE, COR_ROWS), spread_row(SHIFT_LAT)), h_cor[:, lanes])
        lat = dot(rows_of((SHIFT_LAT * ROWS_LON, LAT_ROWS), wide_row), h_lat[:, lanes])
        for row in range(COLS_LAT):
            if row < SHIFT_LAT:
                strip = cor[row * EDGE : (row + 1) * EDGE]
                inner = lat[row * ROWS_LON : (row + 1) * ROWS_LON]
                whole = jnp.concatenate([jnp.where(first, strip, inner[:EDGE]), inner[EDGE:]], 0)
                out[row] = whole.astype(BF16)
            else:
                strip = lon[(row - SHIFT_LAT) * EDGE : (row - SHIFT_LAT + 1) * EDGE]
                inner = own[row - SHIFT_LAT, pl.ds(0, 2 * EDGE), :].astype(F32)
                whole = jnp.concatenate([jnp.where(first, strip, inner[:EDGE]), inner[EDGE:]], 0)
                out[row, pl.ds(0, 2 * EDGE), :] = whole.astype(BF16)


def add_kernel(keep, received, out):
    out[...] = (keep[...].astype(F32) + received[...].astype(F32)).astype(BF16)


def sum_kernel(pieces, out):
    total = pieces[0].astype(F32)
    for piece in range(1, 16):
        total = total + pieces[piece].astype(F32)
    out[...] = total.astype(BF16)


def spread_kernel(piece, received, copies, gain):
    total = (piece[...].astype(F32) + received[...].astype(F32)).astype(BF16)
    gain[...] = total[:, 4 * D :].astype(F32)
    for at in range(16):
        copies[at] = total[:, : 4 * D]


def place_kernel(later, half, grads, *refs):
    gqkv, gproj, wide, square, sems = refs[2:] if later else refs
    copies = []
    for part in range(4):
        rows = pl.ds(part * 64, 64)
        wide[rows, :] = grads[rows, pl.ds(0, 3 * D)].astype(F32)
        square[rows, :] = grads[rows, pl.ds(3 * D, D)].astype(F32)
        there = pl.ds(pl.multiple_of(half[0] * 256 + part * 64, 64), 64)
        for at, (source, out) in enumerate(((wide, gqkv), (square, gproj))):
            copies.append(pltpu.make_async_copy(source.at[rows], out.at[there], sems.at[part, at]))
            copies[-1].start()
    for copy in copies:
        copy.wait()


def place(half, grads, *filled):
    hbm = pl.BlockSpec(memory_space=pl.ANY)
    return pl.pallas_call(
        functools.partial(place_kernel, bool(filled)),
        out_shape=[jax.ShapeDtypeStruct((D, 3 * D), F32), jax.ShapeDtypeStruct((D, D), F32)],
        in_specs=[pl.BlockSpec(memory_space=pltpu.SMEM), pl.BlockSpec(memory_space=pltpu.VMEM)] + [hbm] * len(filled),
        out_specs=[hbm, hbm],
        input_output_aliases={2: 0, 3: 1} if filled else {},
        scratch_shapes=[
            pltpu.VMEM((256, 3 * D), F32),
            pltpu.VMEM((256, D), F32),
            pltpu.SemaphoreType.DMA((4, 2)),
        ],
        compiler_params=pltpu.CompilerParams(vmem_limit_bytes=8 * MIB),
        cost_estimate=pl.CostEstimate(flops=10**6, bytes_accessed=3 * 2**20, transcendentals=0),
        name="place",
    )(half, grads, *filled)


def edges_kernel(where, x_h, g_h, region_h, h_lon, h_lat, h_cor, strips, slabs, region, sems):
    loads = [(region_h, region)]
    for at, ref in enumerate((x_h, g_h)):
        loads += [(ref.at[:, pl.ds(0, 2 * EDGE), :], strips.at[at]), (ref.at[pl.ds(0, SHIFT_LAT)], slabs.at[at])]
    for load in staged(loads, sems):
        load.wait()
    ids = region[...].astype(F32)
    marks = region_marks(ids, range(COLS_LAT))
    strip = jnp.concatenate([marks[lat * ROWS_LON : lat * ROWS_LON + 2 * EDGE] for lat in range(COLS_LAT)], 0)
    width = COLS_LAT * 2 * EDGE
    slab = SHIFT_LAT * ROWS_LON
    for out, rows, at, pick, source in (
        (h_lon, LON_ROWS, LON_IDS, rows_of((LON_ROWS, width), strip_row(SHIFT_LAT, 2 * EDGE)), strip),
        (h_lat, LAT_ROWS, LAT_IDS, rows_of((LAT_ROWS, slab), slab_row), marks[:slab]),
        (h_cor, COR_ROWS, COR_IDS, rows_of((COR_ROWS, width), strip_row(0, 2 * EDGE)), strip),
    ):
        line = jnp.sum(jnp.where(diagonal(rows), dot(pick, source), 0.0), axis=0, keepdims=True)
        line = jnp.concatenate([line] * (D // 128), 1)
        here = lax.broadcasted_iota(jnp.int32, (rows, D), 0) == at
        for array in range(2):
            tokens = slabs[array].reshape(slab, D) if out is h_lat else strips[array].reshape(width, D)
            out[:, pl.ds(array * D, D)] = jnp.where(here, line, dot(pick, tokens)).astype(BF16)


def pass_scratch():
    return [
        pltpu.VMEM((HALF, 3 * D), F32),
        pltpu.VMEM((HALF, D), F32),
        pltpu.VMEM((HALF, 128), F32),
        pltpu.VMEM((HALF, D), F32),
        pltpu.VMEM((HALF, 3 * D), F32),
        pltpu.VMEM((HALF, D), BF16),
        pltpu.VMEM((HALF, D), BF16),
        pltpu.VMEM((HALF, D), BF16),
        pltpu.VMEM((HALF, 3 * D), BF16),
        pltpu.SemaphoreType.DMA((2, 2)),
    ]


def call(kernel, outs, scratch, flops, name, scalars=0, far=0, kept=0, vmem=24):
    def run(*args):
        args = list(args)
        for at in range(scalars, scalars + far):
            args[at] = pltpu.with_memory_space_constraint(args[at], pltpu.HBM)
        specs = [pl.BlockSpec(memory_space=pltpu.SMEM)] * scalars
        specs += [pl.BlockSpec(memory_space=pltpu.HBM)] * far
        specs += [pl.BlockSpec(memory_space=pltpu.VMEM)] * (len(args) - scalars - far)
        return pl.pallas_call(
            kernel,
            out_shape=[pltpu.HBM(*out) if at < kept else jax.ShapeDtypeStruct(*out) for at, out in enumerate(outs)],
            in_specs=specs,
            out_specs=[pl.BlockSpec(memory_space=pltpu.HBM if at < kept else pltpu.VMEM) for at in range(len(outs))],
            scratch_shapes=scratch,
            compiler_params=pltpu.CompilerParams(vmem_limit_bytes=vmem * MIB),
            cost_estimate=pl.CostEstimate(flops=flops, bytes_accessed=8 * 2**20, transcendentals=2**19),
            name=name,
        )(*args)

    return run


def swapped(block, axis, size, bit):
    return lax.ppermute(block, axis, [(i, i ^ bit) for i in range(size)])


def body(tokens, cotangent, region, gain, w_qkv, w_proj):
    x = tokens.transpose(1, 0, 2)
    g = cotangent.transpose(1, 0, 2)
    edges = [((rows, 2 * D), BF16) for rows in (LON_ROWS, LAT_ROWS, COR_ROWS)]
    where = jnp.stack([lax.axis_index("core"), (lax.axis_index(LAT_AXES) == 15).astype(jnp.int32)]).astype(jnp.int32)
    ids = region.T
    scratch = [pltpu.VMEM((2, COLS_LAT, 2 * EDGE, D), BF16), pltpu.VMEM((2, SHIFT_LAT, ROWS_LON, D), BF16)]
    scratch += [pltpu.VMEM((COLS_LAT, ROWS_LON), jnp.int32), pltpu.SemaphoreType.DMA((5,))]
    e_lon, e_lat, e_cor = call(edges_kernel, edges, scratch, 10**6, "edges", 1, far=3, vmem=8)(where, x, g, ids)
    lon_back = [((i + 1) % 16, i) for i in range(16)]
    lat_back = lon_back
    both_back = [(((i + 1) % 16) * 16 + (j + 1) % 16, i * 16 + j) for i in range(16) for j in range(16)]

    h_lon = lax.ppermute(e_lon, LON_AXES, lon_back)
    h_lat = lax.ppermute(e_lat, LAT_AXES, lat_back)
    h_cor = lax.ppermute(e_cor, LON_AXES + LAT_AXES, both_back)

    gain_row = gain.reshape(1, D)
    acts = [((HALF, D), BF16), ((HALF, D), BF16), ((HALF, D), BF16), ((HALF, 3 * D), BF16)]
    constant = functools.partial(jnp.asarray, dtype=BF16)
    weights = [((D, 3 * D), BF16), ((D, D), BF16)]
    picks = [inner_pick(), edge_pick(0), edge_pick(1), last_pick()]
    passed = [((D, 3 * D), F32), ((D, D), F32)] + weights + [(pick.shape, BF16) for pick in picks[1:]]
    passed += [((2, 2 * WIN_LAT, 16, D), BF16), ((2, SHIFT_LAT, ROWS_LON, D), BF16), ((COLS_LAT, ROWS_LON), jnp.int32)]
    slabs = [pltpu.VMEM((2 * WIN_LAT, ROWS_LON, D), BF16)] * 2 + [pltpu.VMEM((3 * WIN, SLAB), BF16)]
    picks = [constant(pick) for pick in picks]
    x1, g1, att1, dp1, *passed = call(
        first_kernel,
        acts + passed,
        pass_scratch() + slabs + [pltpu.SemaphoreType.DMA((13,))],
        4 * 10**9,
        "inner",
        far=9,
        kept=4,
    )(x, g, ids, picks[0], w_qkv, w_proj, *picks[1:], gain_row)

    width = 4 * D + 128
    x2, g2, att2, dp2, keep, send = call(
        second_kernel,
        acts + [((256, width), BF16), ((256, width), BF16)],
        pass_scratch() + [pltpu.VMEM((D, 4 * D), F32)],
        4 * 10**9,
        "outer",
        1,
        kept=4,
    )(where, h_lon, h_lat, h_cor, gain_row, *passed)

    (mine,) = call(add_kernel, [((256, width), BF16)], [], 10**5, "add", vmem=8)(keep, swapped(send, "core", 2, 1))
    mine, x1, x2 = lax.optimization_barrier((mine, x1, x2))
    pieces = lax.all_to_all(mine.reshape(16, 16, -1), PLANE, 0, 0, tiled=True)
    mixed_c, tgrad_c, s_lon, s_lat, s_cor = call(
        third_kernel,
        [((COLS_LAT, ROWS_LON, D), BF16)] * 2
        + edges,
        [pltpu.VMEM((2 * HALF, D), F32)] * 2
        + [pltpu.VMEM((2, HALF, D), BF16)] * 3
        + [pltpu.VMEM((2, HALF, 3 * D), BF16), pltpu.VMEM((SLAB, 4 * WIN), BF16)]
        + [pltpu.VMEM(*weight) for weight in weights]
        + [pltpu.SemaphoreType.DMA((11,))],
        4 * 10**9,
        "tokens",
        far=11,
        vmem=28,
    )(x1, g1, att1, dp1, x2, g2, att2, dp2, constant(slab_place()), w_qkv, w_proj, gain_row)
    lon_on = [(j, i) for i, j in lon_back]
    both_on = [(j, i) for i, j in both_back]
    t_lon = lax.ppermute(s_lon, LON_AXES, lon_on)
    t_lat = lax.ppermute(s_lat, LAT_AXES, lon_on)
    t_cor = lax.ppermute(s_cor, LON_AXES + LAT_AXES, both_on)

    pieces, t_lon, t_lat, t_cor = lax.optimization_barrier((pieces, t_lon, t_lat, t_cor))
    (piece,) = call(sum_kernel, [((16, width), BF16)], [], 10**5, "sum", vmem=8)(pieces)
    for bit in (1, 2):
        (piece,) = call(add_kernel, [((16, width), BF16)], [], 10**5, "add", vmem=4)(piece, swapped(piece, "z", 8, bit))
    copies, gain_tile = call(spread_kernel, [((16, 16, 4 * D), BF16), ((16, 128), F32)], [], 10**5, "spread", vmem=8)(
        piece, swapped(piece, "z", 8, 6)
    )
    gain_grad = gain_tile[:4].reshape(D) / gain
    grads = lax.all_to_all(copies, PLANE, 0, 0, tiled=True)
    mixed, tokens_grad = call(restore_kernel, [((COLS_LAT, ROWS_LON, D), BF16)] * 2, [], 10**6, "restore", vmem=10)(
        mixed_c, tgrad_c, t_lon, t_lat, t_cor
    )
    grads, mixed, tokens_grad = lax.optimization_barrier((grads, mixed, tokens_grad))
    grads = grads.reshape(256, 4 * D)
    other = swapped(grads, "core", 2, 1)
    core = where[:1]
    qkv_grad, proj_grad = place(1 - core, other, *place(core, grads))

    return mixed.transpose(1, 0, 2), tokens_grad.transpose(1, 0, 2), qkv_grad, proj_grad, gain_grad


def solution(mesh):
    fine = Mesh(mesh.devices.reshape(2, 8, 2, 4, 2), ("y_lo", "z", "y_hi", "x", "core"))
    grid = P(LON_AXES, LAT_AXES, None)
    return jax.shard_map(
        body,
        mesh=fine,
        in_specs=(grid, grid, P(LON_AXES, LAT_AXES), P(), P(), P()),
        out_specs=(grid, grid, P(), P(), P()),
        check_vma=False,
    )
```

```python
import functools

import jax
import jax.numpy as jnp
import numpy as np
from jax import lax
from jax.experimental import pallas as pl
from jax.experimental.pallas import tpu as pltpu
from jax.sharding import Mesh, PartitionSpec as P

HEADS = 8
HEAD_DIM = 64
WIN_LON = 12
WIN_LAT = 6
WIN = WIN_LON * WIN_LAT
SHIFT_LON = 6
SHIFT_LAT = 3
D = 512
ROWS_LON = 48
COLS_LAT = 18
SLAB = WIN_LAT * ROWS_LON
EDGE = 8
HALF = 6 * WIN
PIECES = 32
LON_ROWS, LAT_ROWS, COR_ROWS = 96, 128, 32
LON_IDS, LAT_IDS, COR_IDS = 90, 126, 18
F32 = jnp.float32
BF16 = jnp.bfloat16
MIB = 1024 * 1024

PLANE = ("y_lo", "z_lo", "y_hi", "x")
LON_AXES = ("y_lo", "z_hi", "z_lo")
LAT_AXES = ("y_hi", "x", "core")


def window_source(window, row):
    jj, ii = divmod(row, WIN_LON)
    return jj, (window * WIN_LON + ii + SHIFT_LON) % ROWS_LON


def inner_pick():
    out = np.zeros((3 * WIN, SLAB), np.float32)
    for window in range(3):
        for row in range(WIN):
            jj, i = window_source(window, row)
            out[window * WIN + row, jj * ROWS_LON + i] = 1
    return out


def edge_pick(column):
    out = np.zeros((WIN, WIN_LAT * 16 + LON_ROWS), np.float32)
    for row in range(WIN):
        jj, i = window_source(3, row)
        if i >= SHIFT_LON:
            out[row, jj * 16 + i - 32] = 1
        else:
            out[row, WIN_LAT * 16 + (column * WIN_LAT + jj) * SHIFT_LON + i] = 1
    return out


def last_pick():
    own = SHIFT_LAT * ROWS_LON
    out = np.zeros((4 * WIN, own + LAT_ROWS + LON_ROWS + COR_ROWS), np.float32)
    for window in range(4):
        for row in range(WIN):
            jj, i = window_source(window, row)
            if i >= SHIFT_LON and jj < SHIFT_LAT:
                at = jj * ROWS_LON + i
            elif i >= SHIFT_LON:
                at = own + (jj - SHIFT_LAT) * (ROWS_LON - SHIFT_LON) + i - SHIFT_LON
            elif jj < SHIFT_LAT:
                at = own + LAT_ROWS + (2 * WIN_LAT + jj) * SHIFT_LON + i
            else:
                at = own + LAT_ROWS + LON_ROWS + (jj - SHIFT_LAT) * SHIFT_LON + i
            out[window * WIN + row, at] = 1
    return out


def slab_place():
    out = np.zeros((SLAB, 4 * WIN), np.float32)
    for window in range(4):
        for row in range(WIN):
            jj, i = window_source(window, row)
            out[jj * ROWS_LON + i, window * WIN + row] = 1
    return out


def dot(a, b):
    return jnp.dot(a, b, preferred_element_type=F32)


def dot_nt(a, b):
    return lax.dot_general(a, b, (((1,), (1,)), ((), ())), preferred_element_type=F32)


def dot_tn(a, b):
    return lax.dot_general(a, b, (((0,), (0,)), ((), ())), preferred_element_type=F32)


def normalise(x):
    centred = x - jnp.mean(x, axis=-1, keepdims=True)
    variance = jnp.mean(centred * centred, axis=-1, keepdims=True)
    inverse = lax.rsqrt(variance + 1e-05)
    return centred * inverse, inverse


def staged(pairs, sems):
    copies = [pltpu.make_async_copy(source, scratch, sems.at[at]) for at, (source, scratch) in enumerate(pairs)]
    for copy in copies:
        copy.start()
    return copies


def rows_of(shape, where):
    row = lax.broadcasted_iota(jnp.int32, shape, 0)
    return jnp.where(lax.broadcasted_iota(jnp.int32, shape, 1) == where(row), 1.0, 0.0).astype(BF16)


def strip_row(first, pitch):
    def where(row):
        lat = (row * 10923) >> 16
        return (lat + first) * pitch + row - lat * SHIFT_LON

    return where


def slab_row(row):
    lat = (row >= 42).astype(jnp.int32) + (row >= 84).astype(jnp.int32)
    return jnp.where(row < LAT_IDS, lat * ROWS_LON + SHIFT_LON + row - lat * 42, -1)


def spread_row(kept):
    def where(row):
        lat, lon = row >> 3, row & 7
        return jnp.where((lon < SHIFT_LON) & (lat < kept), lat * SHIFT_LON + lon, -1)

    return where


def wide_row(row):
    lat = (row >= 48).astype(jnp.int32) + (row >= 96).astype(jnp.int32)
    lon = row - lat * ROWS_LON
    return jnp.where(lon >= SHIFT_LON, lat * 42 + lon - SHIFT_LON, -1)


def diagonal(rows):
    shape = (rows, 128)
    return lax.broadcasted_iota(jnp.int32, shape, 0) == lax.broadcasted_iota(jnp.int32, shape, 1)


def region_marks(region, lats):
    columns = region.T
    return jnp.concatenate(
        [jnp.broadcast_to(columns[:, lat : lat + 1], (ROWS_LON, 128)) for lat in lats], 0
    ).astype(BF16)


def windows_pass(x_w, g_w, lab_w, gain, wqkv, wproj, att_b, dp_b, proj, gatt, onehot, att, dp):
    normed, _ = normalise(x_w[...].astype(F32))
    hidden = (normed * gain[...]).astype(BF16)
    proj[...] = dot(hidden, wqkv[...])
    gatt[...] = dot_nt(g_w[...], wproj[...])
    lane = lax.broadcasted_iota(jnp.int32, (HALF, 128), 1).astype(F32)
    onehot[...] = jnp.where(lab_w == lane, 1.0, 0.0)
    low = lax.broadcasted_iota(jnp.int32, (WIN, 128), 1) < HEAD_DIM

    def stacked(pair):
        return jnp.concatenate([jnp.where(low, pair, 0.0), jnp.where(low, 0.0, pair)], 0)

    def unstacked(both):
        return jnp.where(low, both[:WIN], both[WIN:])

    def one_window(window):
        rows = pl.ds(window * WIN, WIN)
        marks = onehot[rows, :]
        marks_q = jnp.concatenate([marks, marks], 0).astype(BF16)
        bar_k = ((marks - 1.0) * 1e30).astype(BF16)
        pairs = range(HEADS // 2)
        q, k, v, do = [], [], [], []
        for pair in pairs:
            cols = pl.ds(pair * 128, 128)
            q.append(stacked(proj[rows, pl.ds(pair * 128, 128)].astype(BF16).astype(F32) * HEAD_DIM**-0.5).astype(BF16))
            k.append(proj[rows, pl.ds(D + pair * 128, 128)].astype(BF16))
            v.append(proj[rows, pl.ds(2 * D + pair * 128, 128)].astype(BF16))
            do.append(stacked(gatt[rows, cols]).astype(BF16))
        s = [dot_nt(jnp.concatenate([k[p], bar_k], 1), jnp.concatenate([q[p], marks_q], 1)) for p in pairs]
        da = [dot_nt(v[p], do[p]) for p in pairs]
        a, ab, ds = [], [], []
        for p in pairs:
            lifted = jnp.exp(s[p] - jnp.max(s[p], axis=0, keepdims=True))
            a.append(lifted * (1.0 / jnp.sum(lifted, axis=0, keepdims=True)))
            ab.append(a[p].astype(BF16))
        for p in pairs:
            inner = jnp.sum(da[p] * a[p], axis=0, keepdims=True)
            ds.append((a[p] * (da[p] - inner)).astype(BF16))
        for p in pairs:
            cols = pl.ds(p * 128, 128)
            att[rows, cols] = unstacked(dot_tn(ab[p], v[p]))
            dp[rows, pl.ds(2 * D + p * 128, 128)] = dot(ab[p], do[p])
            dp[rows, cols] = unstacked(dot_tn(ds[p], k[p])) * HEAD_DIM**-0.5
            dp[rows, pl.ds(D + p * 128, 128)] = dot(ds[p], q[p])

    for window in range(6):
        one_window(window)
    att_b[...] = att[...].astype(BF16)
    dp_b[...] = dp[...].astype(BF16)
    return hidden


def first_kernel(
    x, g, wqkv, wproj, pick, region, gain, x_o, g_o, att_o, dp_o, gqkv, gproj,
    proj, gatt, onehot, att, dp, x_w, g_w, att_b, dp_b, out_sems,
):
    ids = region[...].astype(F32)
    parts = {"r": []}
    for column in range(2):
        start = SHIFT_LAT + column * WIN_LAT
        parts["r"].append(dot(pick[...], region_marks(ids, range(start, start + WIN_LAT))))
    parts["r"] = jnp.concatenate(parts["r"], 0)
    for name, ref in (("x", x), ("g", g)):
        got = []
        for column in range(2):
            start = column * WIN_LAT
            got.append(dot(pick[...], ref[start : start + WIN_LAT].reshape(SLAB, D)))
        parts[name] = jnp.concatenate(got, 0)
    x_w[...] = parts["x"].astype(BF16)
    g_w[...] = parts["g"].astype(BF16)
    stores = staged([(x_w, x_o), (g_w, g_o)], out_sems.at[0])
    hidden = windows_pass(x_w, g_w, parts["r"], gain, wqkv, wproj, att_b, dp_b, proj, gatt, onehot, att, dp)
    stores += staged([(att_b, att_o), (dp_b, dp_o)], out_sems.at[1])
    gqkv[...] = dot_tn(hidden, dp_b[...])
    gproj[...] = dot_tn(att_b[...], g_w[...])
    for store in stores:
        store.wait()


def second_kernel(
    where, h_lon, h_lat, h_cor, gain, gqkv1, gproj1, wqkv, wproj, pick0, pick1, pick2, ends, tails, region,
    x_o, g_o, att_o, dp_o, keep, send, proj, gatt, onehot, att, dp, x_w, g_w, att_b, dp_b, out_sems, total,
):
    parts = []
    ids = region[...].astype(F32)
    halos = ((h_lon, LON_ROWS, LON_IDS), (h_lat, LAT_ROWS, LAT_IDS), (h_cor, COR_ROWS, COR_IDS))
    for array in range(3):
        if array == 2:
            halo = []
            for packed, rows, at in halos:
                line = packed[pl.ds(at // 16 * 16, 16), pl.ds(0, 128)].astype(F32)[at % 16 : at % 16 + 1]
                column = jnp.sum(jnp.where(diagonal(rows), line, 0.0), axis=1, keepdims=True)
                halo.append(jnp.broadcast_to(column, (rows, 128)).astype(BF16))
        else:
            halo = [packed[:, pl.ds(array * D, D)] for packed, _, _ in halos]

        got = []
        for column, pick in ((0, pick0), (1, pick1)):
            first = column * WIN_LAT
            if array == 2:
                marks = region_marks(ids, range(SHIFT_LAT + first, SHIFT_LAT + first + WIN_LAT))
                own = jnp.concatenate([marks[lat * ROWS_LON + 32 : (lat + 1) * ROWS_LON] for lat in range(WIN_LAT)], 0)
            else:
                own = ends[array, first : first + WIN_LAT].reshape(WIN_LAT * 16, D)
            got.append(dot(pick[...], jnp.concatenate([own, halo[0]], 0)))
        if array == 2:
            own = region_marks(ids, range(COLS_LAT - SHIFT_LAT, COLS_LAT))
        else:
            own = tails[array].reshape(SHIFT_LAT * ROWS_LON, D)
        got.append(dot(pick2[...], jnp.concatenate([own, halo[1], halo[0], halo[2]], 0)))
        parts.append(jnp.concatenate(got, 0))
    x_w[...] = parts[0].astype(BF16)
    g_w[...] = parts[1].astype(BF16)
    stores = staged([(x_w, x_o), (g_w, g_o)], out_sems.at[0])
    row = lax.broadcasted_iota(jnp.int32, (HALF, 128), 0)
    past = jnp.zeros((HALF, 128), jnp.bool_)
    for window in range(2, 6):
        past = past | ((row >= window * WIN + WIN // 2) & (row < (window + 1) * WIN))
    labels = parts[2] + jnp.where(past, 3.0, 0.0) * where[1].astype(F32)
    hidden = windows_pass(x_w, g_w, labels, gain, wqkv, wproj, att_b, dp_b, proj, gatt, onehot, att, dp)
    stores += staged([(att_b, att_o), (dp_b, dp_o)], out_sems.at[1])
    total[:, pl.ds(0, 3 * D)] = gqkv1[...] + dot_tn(hidden, dp_b[...])
    total[:, pl.ds(3 * D, D)] = gproj1[...] + dot_tn(att_b[...], g_w[...])
    scaled = jnp.sum(total[:, pl.ds(0, 3 * D)] * wqkv[...].astype(F32), axis=1, keepdims=True)
    line = [
        jnp.sum(jnp.where(diagonal(128), scaled[at * 128 : (at + 1) * 128], 0.0), axis=0, keepdims=True) for at in range(4)
    ]
    tile = jnp.concatenate(line + [jnp.zeros((12, 128), F32)], 0).astype(BF16)
    core = where[0]
    for ref, half in ((keep, core), (send, 1 - core)):
        rows = pl.ds(pl.multiple_of(half * 256, 256), 256)
        for side in range(2):
            ref[pl.ds(side * 256, 256), pl.ds(0, 2 * D)] = total[rows, pl.ds(side * 2 * D, 2 * D)].astype(BF16)
        for piece in range(PIECES):
            ref[pl.ds(piece * 16, 16), pl.ds(2 * D, 128)] = tile
    for store in stores:
        store.wait()


def third_kernel(
    x1_h, g1_h, att1_h, dp1_h, x2_h, g2_h, att2_h, dp2_h, place_h, wqkv_h, wproj_h, gain,
    mixed, tgrad, s_lon, s_lat, s_cor, mixed_f, tgrad_f, xs, gs, atts, dps, place, wqkv, wproj, sems,
):
    first = [(wproj_h, wproj), (wqkv_h, wqkv), (x1_h, xs.at[0]), (att1_h, atts.at[0]), (dp1_h, dps.at[0])]
    second = [(g1_h, gs.at[0]), (x2_h, xs.at[1]), (att2_h, atts.at[1]), (dp2_h, dps.at[1]), (g2_h, gs.at[1])]
    loads = staged(first + second + [(place_h, place)], sems)
    for at in range(2):
        for load in loads[:6] if at == 0 else loads[6:]:
            load.wait()
        x, g, att, dp = xs.at[at], gs.at[at], atts.at[at], dps.at[at]
        rows = pl.ds(at * HALF, HALF)
        flat = x[...].astype(F32)
        mixed_f[rows, :] = flat + dot(att[...], wproj[...])
        normed, inverse = normalise(flat)
        grad_normed = dot_nt(dp[...], wqkv[...]) * gain[...]
        grad_input = inverse * (
            grad_normed
            - jnp.mean(grad_normed, axis=-1, keepdims=True)
            - normed * jnp.mean(grad_normed * normed, axis=-1, keepdims=True)
        )
        tgrad_f[rows, :] = g[...].astype(F32) + grad_input
    for at, (ref, out) in enumerate(((mixed_f, mixed), (tgrad_f, tgrad))):
        lanes = pl.ds(at * D, D)
        strips = []
        for column in range(3):
            if column < 2:
                ordered = jnp.concatenate(
                    [ref[pl.ds(column * 3 * WIN, 3 * WIN), :], ref[pl.ds(HALF + column * WIN, WIN), :]], 0
                )
            else:
                ordered = ref[pl.ds(HALF + 2 * WIN, 4 * WIN), :]
            slab = dot(place[...], ordered.astype(BF16)).reshape(WIN_LAT, ROWS_LON, D)
            out[column * WIN_LAT : (column + 1) * WIN_LAT] = slab.astype(BF16)
            strips.append(slab[:, :EDGE].reshape(WIN_LAT * EDGE, D))
        strip = jnp.concatenate(strips, 0).astype(BF16)
        last = slab[SHIFT_LAT:].reshape(SHIFT_LAT * ROWS_LON, D).astype(BF16)
        s_lon[:, lanes] = dot(rows_of((LON_ROWS, COLS_LAT * EDGE), strip_row(0, EDGE)), strip).astype(BF16)
        s_lat[:, lanes] = dot(rows_of((LAT_ROWS, SHIFT_LAT * ROWS_LON), slab_row), last).astype(BF16)
        s_cor[:, lanes] = dot(rows_of((COR_ROWS, COLS_LAT * EDGE), strip_row(15, EDGE)), strip).astype(BF16)


def restore_kernel(mixed_c, tgrad_c, h_lon, h_lat, h_cor, mixed, tgrad):
    kept = COLS_LAT - SHIFT_LAT
    first = lax.broadcasted_iota(jnp.int32, (EDGE, D), 0) < SHIFT_LON
    for at, (own, out) in enumerate(((mixed_c, mixed), (tgrad_c, tgrad))):
        lanes = pl.ds(at * D, D)
        out[SHIFT_LAT:] = own[:kept]
        lon = dot(rows_of((kept * EDGE, LON_ROWS), spread_row(kept)), h_lon[:, lanes])
        cor = dot(rows_of((SHIFT_LAT * EDGE, COR_ROWS), spread_row(SHIFT_LAT)), h_cor[:, lanes])
        lat = dot(rows_of((SHIFT_LAT * ROWS_LON, LAT_ROWS), wide_row), h_lat[:, lanes])
        for row in range(COLS_LAT):
            if row < SHIFT_LAT:
                strip = cor[row * EDGE : (row + 1) * EDGE]
                inner = lat[row * ROWS_LON : (row + 1) * ROWS_LON]
                whole = jnp.concatenate([jnp.where(first, strip, inner[:EDGE]), inner[EDGE:]], 0)
                out[row] = whole.astype(BF16)
            else:
                strip = lon[(row - SHIFT_LAT) * EDGE : (row - SHIFT_LAT + 1) * EDGE]
                inner = own[row - SHIFT_LAT, pl.ds(0, 2 * EDGE), :].astype(F32)
                whole = jnp.concatenate([jnp.where(first, strip, inner[:EDGE]), inner[EDGE:]], 0)
                out[row, pl.ds(0, 2 * EDGE), :] = whole.astype(BF16)


def add_kernel(keep, received, out):
    out[...] = (keep[...].astype(F32) + received[...].astype(F32)).astype(BF16)


def sum_kernel(pieces, out):
    total = pieces[0].astype(F32)
    for piece in range(1, PIECES):
        total = total + pieces[piece].astype(F32)
    out[...] = total.astype(BF16)


def spread_kernel(piece, received, copies, gain):
    total = (piece[...].astype(F32) + received[...].astype(F32)).astype(BF16)
    gain[...] = total[:, 2 * D :].astype(F32)
    for at in range(PIECES):
        copies[at] = total[:, : 2 * D]


def place_kernel(later, half, grads, *refs):
    gqkv, gproj, wide, square, sems = refs[2:] if later else refs
    copies = []
    for part in range(4):
        rows = pl.ds(part * 64, 64)
        right = pl.ds(256 + part * 64, 64)
        wide[rows, pl.ds(0, 2 * D)] = grads[rows, :].astype(F32)
        wide[rows, pl.ds(2 * D, D)] = grads[right, pl.ds(0, D)].astype(F32)
        square[rows, :] = grads[right, pl.ds(D, D)].astype(F32)
        there = pl.ds(pl.multiple_of(half[0] * 256 + part * 64, 64), 64)
        for at, (source, out) in enumerate(((wide, gqkv), (square, gproj))):
            copies.append(pltpu.make_async_copy(source.at[rows], out.at[there], sems.at[part, at]))
            copies[-1].start()
    for copy in copies:
        copy.wait()


def place(half, grads, *filled):
    hbm = pl.BlockSpec(memory_space=pl.ANY)
    return pl.pallas_call(
        functools.partial(place_kernel, bool(filled)),
        out_shape=[jax.ShapeDtypeStruct((D, 3 * D), F32), jax.ShapeDtypeStruct((D, D), F32)],
        in_specs=[pl.BlockSpec(memory_space=pltpu.SMEM), pl.BlockSpec(memory_space=pltpu.VMEM)] + [hbm] * len(filled),
        out_specs=[hbm, hbm],
        input_output_aliases={2: 0, 3: 1} if filled else {},
        scratch_shapes=[
            pltpu.VMEM((256, 3 * D), F32),
            pltpu.VMEM((256, D), F32),
            pltpu.SemaphoreType.DMA((4, 2)),
        ],
        compiler_params=pltpu.CompilerParams(vmem_limit_bytes=8 * MIB),
        cost_estimate=pl.CostEstimate(flops=10**6, bytes_accessed=3 * 2**20, transcendentals=0),
        name="place",
    )(half, grads, *filled)


def edges_kernel(
    where, x_h, g_h, region_h, wqkv_h, wproj_h, pick_h, pick0_h, pick1_h, pick2_h,
    h_lon, h_lat, h_cor, x, g, wqkv, wproj, pick, pick0, pick1, pick2, ends, tails, region, strips, slabs, sems,
):
    lats = pl.ds(SHIFT_LAT, 2 * WIN_LAT)
    end = pl.ds(COLS_LAT - SHIFT_LAT, SHIFT_LAT)
    loads = [(region_h, region)]
    for at, ref in enumerate((x_h, g_h)):
        loads += [(ref.at[:, pl.ds(0, 2 * EDGE), :], strips.at[at]), (ref.at[pl.ds(0, SHIFT_LAT)], slabs.at[at])]
    loads += [(pick_h, pick), (x_h.at[lats], x), (g_h.at[lats], g), (wqkv_h, wqkv), (wproj_h, wproj)]
    loads += [(pick0_h, pick0), (pick1_h, pick1), (pick2_h, pick2)]
    for at, ref in enumerate((x_h, g_h)):
        loads += [(ref.at[lats, pl.ds(32, 16), :], ends.at[at]), (ref.at[end], tails.at[at])]
    loads = staged(loads, sems)
    for load in loads[:5]:
        load.wait()
    ids = region[...].astype(F32)
    marks = region_marks(ids, range(COLS_LAT))
    strip = jnp.concatenate([marks[lat * ROWS_LON : lat * ROWS_LON + 2 * EDGE] for lat in range(COLS_LAT)], 0)
    width = COLS_LAT * 2 * EDGE
    slab = SHIFT_LAT * ROWS_LON
    for out, rows, at, chosen, source in (
        (h_lon, LON_ROWS, LON_IDS, rows_of((LON_ROWS, width), strip_row(SHIFT_LAT, 2 * EDGE)), strip),
        (h_lat, LAT_ROWS, LAT_IDS, rows_of((LAT_ROWS, slab), slab_row), marks[:slab]),
        (h_cor, COR_ROWS, COR_IDS, rows_of((COR_ROWS, width), strip_row(0, 2 * EDGE)), strip),
    ):
        line = jnp.sum(jnp.where(diagonal(rows), dot(chosen, source), 0.0), axis=0, keepdims=True)
        line = jnp.concatenate([line] * (D // 128), 1)
        here = lax.broadcasted_iota(jnp.int32, (rows, D), 0) == at
        for array in range(2):
            tokens = slabs[array].reshape(slab, D) if out is h_lat else strips[array].reshape(width, D)
            out[:, pl.ds(array * D, D)] = jnp.where(here, line, dot(chosen, tokens)).astype(BF16)
    for load in loads[5:]:
        load.wait()


def pass_scratch():
    return [
        pltpu.VMEM((HALF, 3 * D), F32),
        pltpu.VMEM((HALF, D), F32),
        pltpu.VMEM((HALF, 128), F32),
        pltpu.VMEM((HALF, D), F32),
        pltpu.VMEM((HALF, 3 * D), F32),
        pltpu.VMEM((HALF, D), BF16),
        pltpu.VMEM((HALF, D), BF16),
        pltpu.VMEM((HALF, D), BF16),
        pltpu.VMEM((HALF, 3 * D), BF16),
        pltpu.SemaphoreType.DMA((2, 2)),
    ]


def call(kernel, outs, scratch, flops, name, scalars=0, far=0, kept=0, vmem=24):
    def run(*args):
        args = list(args)
        for at in range(scalars, scalars + far):
            args[at] = pltpu.with_memory_space_constraint(args[at], pltpu.HBM)
        specs = [pl.BlockSpec(memory_space=pltpu.SMEM)] * scalars
        specs += [pl.BlockSpec(memory_space=pltpu.HBM)] * far
        specs += [pl.BlockSpec(memory_space=pltpu.VMEM)] * (len(args) - scalars - far)
        return pl.pallas_call(
            kernel,
            out_shape=[pltpu.HBM(*out) if at < kept else jax.ShapeDtypeStruct(*out) for at, out in enumerate(outs)],
            in_specs=specs,
            out_specs=[pl.BlockSpec(memory_space=pltpu.HBM if at < kept else pltpu.VMEM) for at in range(len(outs))],
            scratch_shapes=scratch,
            compiler_params=pltpu.CompilerParams(vmem_limit_bytes=vmem * MIB),
            cost_estimate=pl.CostEstimate(flops=flops, bytes_accessed=8 * 2**20, transcendentals=2**19),
            name=name,
        )(*args)

    return run


def swapped(block, axis, size, bit):
    return lax.ppermute(block, axis, [(i, i ^ bit) for i in range(size)])


def body(tokens, cotangent, region, gain, w_qkv, w_proj):
    x = tokens.transpose(1, 0, 2)
    g = cotangent.transpose(1, 0, 2)
    edges = [((rows, 2 * D), BF16) for rows in (LON_ROWS, LAT_ROWS, COR_ROWS)]
    where = jnp.stack([lax.axis_index("core"), (lax.axis_index(LAT_AXES) == 15).astype(jnp.int32)]).astype(jnp.int32)
    constant = functools.partial(jnp.asarray, dtype=BF16)
    picks = [inner_pick(), edge_pick(0), edge_pick(1), last_pick()]
    weights = [((D, 3 * D), BF16), ((D, D), BF16)]
    slab = ((2 * WIN_LAT, ROWS_LON, D), BF16)
    loaded = [slab, slab] + weights + [(pick.shape, BF16) for pick in picks]
    loaded += [((2, 2 * WIN_LAT, 16, D), BF16), ((2, SHIFT_LAT, ROWS_LON, D), BF16), ((COLS_LAT, ROWS_LON), jnp.int32)]
    scratch = [pltpu.VMEM((2, COLS_LAT, 2 * EDGE, D), BF16), pltpu.VMEM((2, SHIFT_LAT, ROWS_LON, D), BF16)]
    scratch += [pltpu.SemaphoreType.DMA((17,))]
    e_lon, e_lat, e_cor, x_s, g_s, wqkv_s, wproj_s, pick, pick0, pick1, pick2, ends, tails, ids = call(
        edges_kernel, edges + loaded, scratch, 10**6, "edges", 1, far=9, vmem=12
    )(where, x, g, region.T, w_qkv, w_proj, *[constant(pick) for pick in picks])
    lon_back = [((i + 1) % 16, i) for i in range(16)]
    lat_back = lon_back
    both_back = [(((i + 1) % 16) * 16 + (j + 1) % 16, i * 16 + j) for i in range(16) for j in range(16)]
    h_lon = lax.ppermute(e_lon, LON_AXES, lon_back)
    h_lat = lax.ppermute(e_lat, LAT_AXES, lat_back)
    h_cor = lax.ppermute(e_cor, LON_AXES + LAT_AXES, both_back)

    gain_row = gain.reshape(1, D)
    acts = [((HALF, D), BF16), ((HALF, D), BF16), ((HALF, D), BF16), ((HALF, 3 * D), BF16)]
    x1, g1, att1, dp1, gqkv1, gproj1 = call(
        first_kernel, acts + [((D, 3 * D), F32), ((D, D), F32)], pass_scratch(), 4 * 10**9, "inner", kept=4
    )(x_s, g_s, wqkv_s, wproj_s, pick, ids, gain_row)

    width = 2 * D + 128
    x2, g2, att2, dp2, keep, send = call(
        second_kernel,
        acts + [((16 * PIECES, width), BF16)] * 2,
        pass_scratch() + [pltpu.VMEM((D, 4 * D), F32)],
        4 * 10**9,
        "outer",
        1,
        kept=4,
    )(
        where, h_lon, h_lat, h_cor, gain_row, gqkv1, gproj1, wqkv_s, wproj_s, pick0, pick1, pick2, ends, tails, ids
    )

    (mine,) = call(add_kernel, [((16 * PIECES, width), BF16)], [], 10**5, "add", vmem=8)(keep, swapped(send, "core", 2, 1))
    mine, x1, x2 = lax.optimization_barrier((mine, x1, x2))
    pieces = lax.all_to_all(mine.reshape(PIECES, 16, -1), PLANE, 0, 0, tiled=True)
    mixed_c, tgrad_c, s_lon, s_lat, s_cor = call(
        third_kernel,
        [((COLS_LAT, ROWS_LON, D), BF16)] * 2
        + edges,
        [pltpu.VMEM((2 * HALF, D), F32)] * 2
        + [pltpu.VMEM((2, HALF, D), BF16)] * 3
        + [pltpu.VMEM((2, HALF, 3 * D), BF16), pltpu.VMEM((SLAB, 4 * WIN), BF16)]
        + [pltpu.VMEM(*weight) for weight in weights]
        + [pltpu.SemaphoreType.DMA((11,))],
        4 * 10**9,
        "tokens",
        far=11,
        vmem=28,
    )(x1, g1, att1, dp1, x2, g2, att2, dp2, constant(slab_place()), w_qkv, w_proj, gain_row)
    lon_on = [(j, i) for i, j in lon_back]
    both_on = [(j, i) for i, j in both_back]
    t_lon = lax.ppermute(s_lon, LON_AXES, lon_on)
    t_lat = lax.ppermute(s_lat, LAT_AXES, lon_on)
    t_cor = lax.ppermute(s_cor, LON_AXES + LAT_AXES, both_on)

    pieces, t_lon, t_lat, t_cor = lax.optimization_barrier((pieces, t_lon, t_lat, t_cor))
    (piece,) = call(sum_kernel, [((16, width), BF16)], [], 10**5, "sum", vmem=8)(pieces)
    (piece,) = call(add_kernel, [((16, width), BF16)], [], 10**5, "add", vmem=4)(piece, swapped(piece, "z_hi", 4, 1))
    copies, gain_tile = call(
        spread_kernel, [((PIECES, 16, 2 * D), BF16), ((16, 128), F32)], [], 10**5, "spread", vmem=8
    )(piece, swapped(piece, "z_hi", 4, 3))
    gain_grad = gain_tile[:4].reshape(D) / gain
    grads = lax.all_to_all(copies, PLANE, 0, 0, tiled=True)
    mixed, tokens_grad = call(restore_kernel, [((COLS_LAT, ROWS_LON, D), BF16)] * 2, [], 10**6, "restore", vmem=10)(
        mixed_c, tgrad_c, t_lon, t_lat, t_cor
    )
    grads, mixed, tokens_grad = lax.optimization_barrier((grads, mixed, tokens_grad))
    grads = grads.reshape(16 * PIECES, 2 * D)
    other = swapped(grads, "core", 2, 1)
    core = where[:1]
    qkv_grad, proj_grad = place(1 - core, other, *place(core, grads))

    return mixed.transpose(1, 0, 2), tokens_grad.transpose(1, 0, 2), qkv_grad, proj_grad, gain_grad


def solution(mesh):
    fine = Mesh(mesh.devices.reshape(2, 4, 2, 2, 4, 2), ("y_lo", "z_hi", "z_lo", "y_hi", "x", "core"))
    grid = P(LON_AXES, LAT_AXES, None)
    return jax.shard_map(
        body,
        mesh=fine,
        in_specs=(grid, grid, P(LON_AXES, LAT_AXES), P(), P(), P()),
        out_specs=(grid, grid, P(), P(), P()),
        check_vma=False,
    )
```

```python
import functools

import jax
import jax.numpy as jnp
import numpy as np
from jax import lax
from jax.experimental import pallas as pl
from jax.experimental.pallas import tpu as pltpu
from jax.sharding import Mesh, PartitionSpec as P

HEADS = 8
HEAD_DIM = 64
WIN_LON = 12
WIN_LAT = 6
WIN = WIN_LON * WIN_LAT
SHIFT_LON = 6
SHIFT_LAT = 3
D = 512
ROWS_LON = 48
COLS_LAT = 18
SLAB = WIN_LAT * ROWS_LON
EDGE = 8
HALF = 6 * WIN
PIECES = 32
LON_ROWS, LAT_ROWS, COR_ROWS = 96, 128, 32
LON_IDS, LAT_IDS, COR_IDS = 90, 126, 18
F32 = jnp.float32
BF16 = jnp.bfloat16
MIB = 1024 * 1024

PLANE = ("y_lo", "z_lo", "y_hi", "x")
LON_AXES = ("y_lo", "z_hi", "z_lo")
LAT_AXES = ("y_hi", "x", "core")


def window_source(window, row):
    jj, ii = divmod(row, WIN_LON)
    return jj, (window * WIN_LON + ii + SHIFT_LON) % ROWS_LON


def inner_pick():
    out = np.zeros((3 * WIN, SLAB), np.float32)
    for window in range(3):
        for row in range(WIN):
            jj, i = window_source(window, row)
            out[window * WIN + row, jj * ROWS_LON + i] = 1
    return out


def edge_pick(column):
    out = np.zeros((WIN, WIN_LAT * 16 + LON_ROWS), np.float32)
    for row in range(WIN):
        jj, i = window_source(3, row)
        if i >= SHIFT_LON:
            out[row, jj * 16 + i - 32] = 1
        else:
            out[row, WIN_LAT * 16 + (column * WIN_LAT + jj) * SHIFT_LON + i] = 1
    return out


def last_pick():
    own = SHIFT_LAT * ROWS_LON
    out = np.zeros((4 * WIN, own + LAT_ROWS + LON_ROWS + COR_ROWS), np.float32)
    for window in range(4):
        for row in range(WIN):
            jj, i = window_source(window, row)
            if i >= SHIFT_LON and jj < SHIFT_LAT:
                at = jj * ROWS_LON + i
            elif i >= SHIFT_LON:
                at = own + (jj - SHIFT_LAT) * (ROWS_LON - SHIFT_LON) + i - SHIFT_LON
            elif jj < SHIFT_LAT:
                at = own + LAT_ROWS + (2 * WIN_LAT + jj) * SHIFT_LON + i
            else:
                at = own + LAT_ROWS + LON_ROWS + (jj - SHIFT_LAT) * SHIFT_LON + i
            out[window * WIN + row, at] = 1
    return out


def slab_place():
    out = np.zeros((SLAB, 4 * WIN), np.float32)
    for window in range(4):
        for row in range(WIN):
            jj, i = window_source(window, row)
            out[jj * ROWS_LON + i, window * WIN + row] = 1
    return out


def dot(a, b):
    return jnp.dot(a, b, preferred_element_type=F32)


def dot_nt(a, b):
    return lax.dot_general(a, b, (((1,), (1,)), ((), ())), preferred_element_type=F32)


def dot_tn(a, b):
    return lax.dot_general(a, b, (((0,), (0,)), ((), ())), preferred_element_type=F32)


def normalise(x):
    centred = x - jnp.mean(x, axis=-1, keepdims=True)
    variance = jnp.mean(centred * centred, axis=-1, keepdims=True)
    inverse = lax.rsqrt(variance + 1e-05)
    return centred * inverse, inverse


def staged(pairs, sems):
    copies = [pltpu.make_async_copy(source, scratch, sems.at[at]) for at, (source, scratch) in enumerate(pairs)]
    for copy in copies:
        copy.start()
    return copies


def rows_of(shape, where):
    row = lax.broadcasted_iota(jnp.int32, shape, 0)
    return jnp.where(lax.broadcasted_iota(jnp.int32, shape, 1) == where(row), 1.0, 0.0).astype(BF16)


def strip_row(first, pitch):
    def where(row):
        lat = (row * 10923) >> 16
        return (lat + first) * pitch + row - lat * SHIFT_LON

    return where


def slab_row(row):
    lat = (row >= 42).astype(jnp.int32) + (row >= 84).astype(jnp.int32)
    return jnp.where(row < LAT_IDS, lat * ROWS_LON + SHIFT_LON + row - lat * 42, -1)


def spread_row(kept):
    def where(row):
        lat, lon = row >> 3, row & 7
        return jnp.where((lon < SHIFT_LON) & (lat < kept), lat * SHIFT_LON + lon, -1)

    return where


def wide_row(row):
    lat = (row >= 48).astype(jnp.int32) + (row >= 96).astype(jnp.int32)
    lon = row - lat * ROWS_LON
    return jnp.where(lon >= SHIFT_LON, lat * 42 + lon - SHIFT_LON, -1)


def diagonal(rows):
    shape = (rows, 128)
    return lax.broadcasted_iota(jnp.int32, shape, 0) == lax.broadcasted_iota(jnp.int32, shape, 1)


def region_marks(region, lats):
    columns = region.T
    return jnp.concatenate(
        [jnp.broadcast_to(columns[:, lat : lat + 1], (ROWS_LON, 128)) for lat in lats], 0
    ).astype(BF16)


def windows_pass(
    x_w, g_w, lab_w, gain, wqkv, wproj, att_o, dp_o, att_b, dp_b, stores, out_sems, proj, gatt, onehot, att, dp
):
    normed, _ = normalise(x_w[...].astype(F32))
    hidden = (normed * gain[...]).astype(BF16)
    proj[...] = dot(hidden, wqkv[...])
    gatt[...] = dot_nt(g_w[...], wproj[...])
    lane = lax.broadcasted_iota(jnp.int32, (HALF, 128), 1).astype(F32)
    onehot[...] = jnp.where(lab_w == lane, 1.0, 0.0)
    low = lax.broadcasted_iota(jnp.int32, (WIN, 128), 1) < HEAD_DIM

    def stacked(pair):
        return jnp.concatenate([jnp.where(low, pair, 0.0), jnp.where(low, 0.0, pair)], 0)

    def unstacked(both):
        return jnp.where(low, both[:WIN], both[WIN:])

    def one_window(window):
        rows = pl.ds(window * WIN, WIN)
        marks = onehot[rows, :]
        marks_q = jnp.concatenate([marks, marks], 0).astype(BF16)
        bar_k = ((marks - 1.0) * 1e30).astype(BF16)
        pairs = range(HEADS // 2)
        q, k, v, do = [], [], [], []
        for pair in pairs:
            cols = pl.ds(pair * 128, 128)
            q.append(stacked(proj[rows, pl.ds(pair * 128, 128)].astype(BF16).astype(F32) * HEAD_DIM**-0.5).astype(BF16))
            k.append(proj[rows, pl.ds(D + pair * 128, 128)].astype(BF16))
            v.append(proj[rows, pl.ds(2 * D + pair * 128, 128)].astype(BF16))
            do.append(stacked(gatt[rows, cols]).astype(BF16))
        s = [dot_nt(jnp.concatenate([k[p], bar_k], 1), jnp.concatenate([q[p], marks_q], 1)) for p in pairs]
        da = [dot_nt(v[p], do[p]) for p in pairs]
        a, ab, ds = [], [], []
        for p in pairs:
            lifted = jnp.exp(s[p] - jnp.max(s[p], axis=0, keepdims=True))
            a.append(lifted * (1.0 / jnp.sum(lifted, axis=0, keepdims=True)))
            ab.append(a[p].astype(BF16))
        for p in pairs:
            inner = jnp.sum(da[p] * a[p], axis=0, keepdims=True)
            ds.append((a[p] * (da[p] - inner)).astype(BF16))
        for p in pairs:
            cols = pl.ds(p * 128, 128)
            att[rows, cols] = unstacked(dot_tn(ab[p], v[p]))
            dp[rows, pl.ds(2 * D + p * 128, 128)] = dot(ab[p], do[p])
            dp[rows, cols] = unstacked(dot_tn(ds[p], k[p])) * HEAD_DIM**-0.5
            dp[rows, pl.ds(D + p * 128, 128)] = dot(ds[p], q[p])

    for window in range(6):
        one_window(window)
        if window % 2:
            rows = pl.ds((window - 1) * WIN, 2 * WIN)
            att_b[rows, :] = att[rows, :].astype(BF16)
            dp_b[rows, :] = dp[rows, :].astype(BF16)
            pairs = [(att_b.at[rows], att_o.at[rows]), (dp_b.at[rows], dp_o.at[rows])]
            stores.extend(staged(pairs, out_sems.at[1 + window // 2]))
    return hidden


def first_kernel(
    x, g, wqkv, wproj, pick, region, gain, x_o, g_o, att_o, dp_o, gqkv, gproj,
    proj, gatt, onehot, att, dp, x_w, g_w, att_b, dp_b, out_sems,
):
    ids = region[...].astype(F32)
    parts = {"r": []}
    for column in range(2):
        start = SHIFT_LAT + column * WIN_LAT
        parts["r"].append(dot(pick[...], region_marks(ids, range(start, start + WIN_LAT))))
    parts["r"] = jnp.concatenate(parts["r"], 0)
    for name, ref in (("x", x), ("g", g)):
        got = []
        for column in range(2):
            start = column * WIN_LAT
            got.append(dot(pick[...], ref[start : start + WIN_LAT].reshape(SLAB, D)))
        parts[name] = jnp.concatenate(got, 0)
    x_w[...] = parts["x"].astype(BF16)
    g_w[...] = parts["g"].astype(BF16)
    stores = staged([(x_w, x_o), (g_w, g_o)], out_sems.at[0])
    hidden = windows_pass(
        x_w, g_w, parts["r"], gain, wqkv, wproj, att_o, dp_o, att_b, dp_b, stores, out_sems, proj, gatt, onehot, att, dp
    )
    gqkv[...] = dot_tn(hidden, dp_b[...])
    gproj[...] = dot_tn(att_b[...], g_w[...])
    for store in stores:
        store.wait()


def second_kernel(
    where, h_lon, h_lat, h_cor, gain, gqkv1, gproj1, wqkv, wproj, pick0, pick1, pick2, ends, tails, region,
    x_o, g_o, att_o, dp_o, keep, send, proj, gatt, onehot, att, dp, x_w, g_w, att_b, dp_b, out_sems, total,
):
    parts = []
    ids = region[...].astype(F32)
    halos = ((h_lon, LON_ROWS, LON_IDS), (h_lat, LAT_ROWS, LAT_IDS), (h_cor, COR_ROWS, COR_IDS))
    for array in range(3):
        if array == 2:
            halo = []
            for packed, rows, at in halos:
                line = packed[pl.ds(at // 16 * 16, 16), pl.ds(0, 128)].astype(F32)[at % 16 : at % 16 + 1]
                column = jnp.sum(jnp.where(diagonal(rows), line, 0.0), axis=1, keepdims=True)
                halo.append(jnp.broadcast_to(column, (rows, 128)).astype(BF16))
        else:
            halo = [packed[:, pl.ds(array * D, D)] for packed, _, _ in halos]

        got = []
        for column, pick in ((0, pick0), (1, pick1)):
            first = column * WIN_LAT
            if array == 2:
                marks = region_marks(ids, range(SHIFT_LAT + first, SHIFT_LAT + first + WIN_LAT))
                own = jnp.concatenate([marks[lat * ROWS_LON + 32 : (lat + 1) * ROWS_LON] for lat in range(WIN_LAT)], 0)
            else:
                own = ends[array, first : first + WIN_LAT].reshape(WIN_LAT * 16, D)
            got.append(dot(pick[...], jnp.concatenate([own, halo[0]], 0)))
        if array == 2:
            own = region_marks(ids, range(COLS_LAT - SHIFT_LAT, COLS_LAT))
        else:
            own = tails[array].reshape(SHIFT_LAT * ROWS_LON, D)
        got.append(dot(pick2[...], jnp.concatenate([own, halo[1], halo[0], halo[2]], 0)))
        parts.append(jnp.concatenate(got, 0))
    x_w[...] = parts[0].astype(BF16)
    g_w[...] = parts[1].astype(BF16)
    stores = staged([(x_w, x_o), (g_w, g_o)], out_sems.at[0])
    row = lax.broadcasted_iota(jnp.int32, (HALF, 128), 0)
    past = jnp.zeros((HALF, 128), jnp.bool_)
    for window in range(2, 6):
        past = past | ((row >= window * WIN + WIN // 2) & (row < (window + 1) * WIN))
    labels = parts[2] + jnp.where(past, 3.0, 0.0) * where[1].astype(F32)
    hidden = windows_pass(
        x_w, g_w, labels, gain, wqkv, wproj, att_o, dp_o, att_b, dp_b, stores, out_sems, proj, gatt, onehot, att, dp
    )
    total[:, pl.ds(0, 3 * D)] = gqkv1[...] + dot_tn(hidden, dp_b[...])
    total[:, pl.ds(3 * D, D)] = gproj1[...] + dot_tn(att_b[...], g_w[...])
    scaled = jnp.sum(total[:, pl.ds(0, 3 * D)] * wqkv[...].astype(F32), axis=1, keepdims=True)
    line = [
        jnp.sum(jnp.where(diagonal(128), scaled[at * 128 : (at + 1) * 128], 0.0), axis=0, keepdims=True) for at in range(4)
    ]
    tile = jnp.concatenate(line + [jnp.zeros((12, 128), F32)], 0).astype(BF16)
    core = where[0]
    for ref, half in ((keep, core), (send, 1 - core)):
        rows = pl.ds(pl.multiple_of(half * 256, 256), 256)
        for side in range(2):
            ref[pl.ds(side * 256, 256), pl.ds(0, 2 * D)] = total[rows, pl.ds(side * 2 * D, 2 * D)].astype(BF16)
        for piece in range(PIECES):
            ref[pl.ds(piece * 16, 16), pl.ds(2 * D, 128)] = tile
    for store in stores:
        store.wait()


def third_kernel(
    x1_h, g1_h, att1_h, dp1_h, x2_h, g2_h, att2_h, dp2_h, place_h, wqkv_h, wproj_h, gain,
    mixed, tgrad, s_lon, s_lat, s_cor, mixed_f, tgrad_f, xs, gs, atts, dps, place, wqkv, wproj, sems,
):
    first = [(wproj_h, wproj), (wqkv_h, wqkv), (x1_h, xs.at[0]), (att1_h, atts.at[0]), (dp1_h, dps.at[0])]
    second = [(g1_h, gs.at[0]), (x2_h, xs.at[1]), (att2_h, atts.at[1]), (dp2_h, dps.at[1]), (g2_h, gs.at[1])]
    loads = staged(first + second + [(place_h, place)], sems)
    for at in range(2):
        for load in loads[:6] if at == 0 else loads[6:]:
            load.wait()
        x, g, att, dp = xs.at[at], gs.at[at], atts.at[at], dps.at[at]
        rows = pl.ds(at * HALF, HALF)
        flat = x[...].astype(F32)
        mixed_f[rows, :] = flat + dot(att[...], wproj[...])
        normed, inverse = normalise(flat)
        grad_normed = dot_nt(dp[...], wqkv[...]) * gain[...]
        grad_input = inverse * (
            grad_normed
            - jnp.mean(grad_normed, axis=-1, keepdims=True)
            - normed * jnp.mean(grad_normed * normed, axis=-1, keepdims=True)
        )
        tgrad_f[rows, :] = g[...].astype(F32) + grad_input
    for at, (ref, out) in enumerate(((mixed_f, mixed), (tgrad_f, tgrad))):
        lanes = pl.ds(at * D, D)
        strips = []
        for column in range(3):
            if column < 2:
                ordered = jnp.concatenate(
                    [ref[pl.ds(column * 3 * WIN, 3 * WIN), :], ref[pl.ds(HALF + column * WIN, WIN), :]], 0
                )
            else:
                ordered = ref[pl.ds(HALF + 2 * WIN, 4 * WIN), :]
            slab = dot(place[...], ordered.astype(BF16)).reshape(WIN_LAT, ROWS_LON, D)
            out[column * WIN_LAT : (column + 1) * WIN_LAT] = slab.astype(BF16)
            strips.append(slab[:, :EDGE].reshape(WIN_LAT * EDGE, D))
        strip = jnp.concatenate(strips, 0).astype(BF16)
        last = slab[SHIFT_LAT:].reshape(SHIFT_LAT * ROWS_LON, D).astype(BF16)
        s_lon[:, lanes] = dot(rows_of((LON_ROWS, COLS_LAT * EDGE), strip_row(0, EDGE)), strip).astype(BF16)
        s_lat[:, lanes] = dot(rows_of((LAT_ROWS, SHIFT_LAT * ROWS_LON), slab_row), last).astype(BF16)
        s_cor[:, lanes] = dot(rows_of((COR_ROWS, COLS_LAT * EDGE), strip_row(15, EDGE)), strip).astype(BF16)


def restore_kernel(mixed_c, tgrad_c, h_lon, h_lat, h_cor, mixed, tgrad):
    kept = COLS_LAT - SHIFT_LAT
    first = lax.broadcasted_iota(jnp.int32, (EDGE, D), 0) < SHIFT_LON
    for at, (own, out) in enumerate(((mixed_c, mixed), (tgrad_c, tgrad))):
        lanes = pl.ds(at * D, D)
        out[SHIFT_LAT:] = own[:kept]
        lon = dot(rows_of((kept * EDGE, LON_ROWS), spread_row(kept)), h_lon[:, lanes])
        cor = dot(rows_of((SHIFT_LAT * EDGE, COR_ROWS), spread_row(SHIFT_LAT)), h_cor[:, lanes])
        lat = dot(rows_of((SHIFT_LAT * ROWS_LON, LAT_ROWS), wide_row), h_lat[:, lanes])
        for row in range(COLS_LAT):
            if row < SHIFT_LAT:
                strip = cor[row * EDGE : (row + 1) * EDGE]
                inner = lat[row * ROWS_LON : (row + 1) * ROWS_LON]
                whole = jnp.concatenate([jnp.where(first, strip, inner[:EDGE]), inner[EDGE:]], 0)
                out[row] = whole.astype(BF16)
            else:
                strip = lon[(row - SHIFT_LAT) * EDGE : (row - SHIFT_LAT + 1) * EDGE]
                inner = own[row - SHIFT_LAT, pl.ds(0, 2 * EDGE), :].astype(F32)
                whole = jnp.concatenate([jnp.where(first, strip, inner[:EDGE]), inner[EDGE:]], 0)
                out[row, pl.ds(0, 2 * EDGE), :] = whole.astype(BF16)


def add_kernel(keep, received, out):
    out[...] = (keep[...].astype(F32) + received[...].astype(F32)).astype(BF16)


def add_out_kernel(keep, received, out, total, sems):
    copies = []
    for part in range(8):
        rows = pl.ds(part * 64, 64)
        total[rows, :] = (keep[rows, :].astype(F32) + received[rows, :].astype(F32)).astype(BF16)
        copies.append(pltpu.make_async_copy(total.at[rows], out.at[rows], sems.at[part]))
        copies[-1].start()
    for copy in copies:
        copy.wait()


def sum_kernel(pieces, out):
    total = pieces[0].astype(F32)
    for piece in range(1, PIECES):
        total = total + pieces[piece].astype(F32)
    out[...] = total.astype(BF16)


def spread_kernel(piece, received, copies, gain, total, sems):
    both = piece[...].astype(F32) + received[...].astype(F32)
    total[...] = both[:, : 2 * D].astype(BF16)
    sent = staged([(total, copies.at[at]) for at in range(PIECES)], sems)
    gain[...] = both[:, 2 * D :].astype(BF16).astype(F32)
    for copy in sent:
        copy.wait()


def place_kernel(later, half, grads, *refs):
    gqkv, gproj, wide, square, sems = refs[2:] if later else refs
    copies = []
    for part in range(4):
        rows = pl.ds(part * 64, 64)
        right = pl.ds(256 + part * 64, 64)
        wide[rows, pl.ds(0, 2 * D)] = grads[rows, :].astype(F32)
        wide[rows, pl.ds(2 * D, D)] = grads[right, pl.ds(0, D)].astype(F32)
        square[rows, :] = grads[right, pl.ds(D, D)].astype(F32)
        there = pl.ds(pl.multiple_of(half[0] * 256 + part * 64, 64), 64)
        for at, (source, out) in enumerate(((wide, gqkv), (square, gproj))):
            copies.append(pltpu.make_async_copy(source.at[rows], out.at[there], sems.at[part, at]))
            copies[-1].start()
    for copy in copies:
        copy.wait()


def place(half, grads, *filled):
    hbm = pl.BlockSpec(memory_space=pl.ANY)
    return pl.pallas_call(
        functools.partial(place_kernel, bool(filled)),
        out_shape=[jax.ShapeDtypeStruct((D, 3 * D), F32), jax.ShapeDtypeStruct((D, D), F32)],
        in_specs=[pl.BlockSpec(memory_space=pltpu.SMEM), pl.BlockSpec(memory_space=pltpu.VMEM)] + [hbm] * len(filled),
        out_specs=[hbm, hbm],
        input_output_aliases={2: 0, 3: 1} if filled else {},
        scratch_shapes=[
            pltpu.VMEM((256, 3 * D), F32),
            pltpu.VMEM((256, D), F32),
            pltpu.SemaphoreType.DMA((4, 2)),
        ],
        compiler_params=pltpu.CompilerParams(vmem_limit_bytes=8 * MIB),
        cost_estimate=pl.CostEstimate(flops=10**6, bytes_accessed=3 * 2**20, transcendentals=0),
        name="place",
    )(half, grads, *filled)


def edges_kernel(
    where, x_h, g_h, region_h, wqkv_h, wproj_h, pick_h, pick0_h, pick1_h, pick2_h,
    h_lon, h_lat, h_cor, x, g, wqkv, wproj, pick, pick0, pick1, pick2, ends, tails, region, strips, slabs, sems,
):
    lats = pl.ds(SHIFT_LAT, 2 * WIN_LAT)
    end = pl.ds(COLS_LAT - SHIFT_LAT, SHIFT_LAT)
    loads = [(region_h, region)]
    for at, ref in enumerate((x_h, g_h)):
        loads += [(ref.at[:, pl.ds(0, 2 * EDGE), :], strips.at[at]), (ref.at[pl.ds(0, SHIFT_LAT)], slabs.at[at])]
    loads += [(pick_h, pick), (x_h.at[lats], x), (g_h.at[lats], g), (wqkv_h, wqkv), (wproj_h, wproj)]
    loads += [(pick0_h, pick0), (pick1_h, pick1), (pick2_h, pick2)]
    for at, ref in enumerate((x_h, g_h)):
        loads += [(ref.at[lats, pl.ds(32, 16), :], ends.at[at]), (ref.at[end], tails.at[at])]
    loads = staged(loads, sems)
    for load in loads[:5]:
        load.wait()
    ids = region[...].astype(F32)
    marks = region_marks(ids, range(COLS_LAT))
    strip = jnp.concatenate([marks[lat * ROWS_LON : lat * ROWS_LON + 2 * EDGE] for lat in range(COLS_LAT)], 0)
    width = COLS_LAT * 2 * EDGE
    slab = SHIFT_LAT * ROWS_LON
    for out, rows, at, chosen, source in (
        (h_lon, LON_ROWS, LON_IDS, rows_of((LON_ROWS, width), strip_row(SHIFT_LAT, 2 * EDGE)), strip),
        (h_lat, LAT_ROWS, LAT_IDS, rows_of((LAT_ROWS, slab), slab_row), marks[:slab]),
        (h_cor, COR_ROWS, COR_IDS, rows_of((COR_ROWS, width), strip_row(0, 2 * EDGE)), strip),
    ):
        line = jnp.sum(jnp.where(diagonal(rows), dot(chosen, source), 0.0), axis=0, keepdims=True)
        line = jnp.concatenate([line] * (D // 128), 1)
        here = lax.broadcasted_iota(jnp.int32, (rows, D), 0) == at
        for array in range(2):
            tokens = slabs[array].reshape(slab, D) if out is h_lat else strips[array].reshape(width, D)
            out[:, pl.ds(array * D, D)] = jnp.where(here, line, dot(chosen, tokens)).astype(BF16)
    for load in loads[5:]:
        load.wait()


def pass_scratch():
    return [
        pltpu.VMEM((HALF, 3 * D), F32),
        pltpu.VMEM((HALF, D), F32),
        pltpu.VMEM((HALF, 128), F32),
        pltpu.VMEM((HALF, D), F32),
        pltpu.VMEM((HALF, 3 * D), F32),
        pltpu.VMEM((HALF, D), BF16),
        pltpu.VMEM((HALF, D), BF16),
        pltpu.VMEM((HALF, D), BF16),
        pltpu.VMEM((HALF, 3 * D), BF16),
        pltpu.SemaphoreType.DMA((4, 2)),
    ]


def call(kernel, outs, scratch, flops, name, scalars=0, far=0, kept=0, vmem=24):
    def run(*args):
        args = list(args)
        for at in range(scalars, scalars + far):
            args[at] = pltpu.with_memory_space_constraint(args[at], pltpu.HBM)
        specs = [pl.BlockSpec(memory_space=pltpu.SMEM)] * scalars
        specs += [pl.BlockSpec(memory_space=pltpu.HBM)] * far
        specs += [pl.BlockSpec(memory_space=pltpu.VMEM)] * (len(args) - scalars - far)
        return pl.pallas_call(
            kernel,
            out_shape=[pltpu.HBM(*out) if at < kept else jax.ShapeDtypeStruct(*out) for at, out in enumerate(outs)],
            in_specs=specs,
            out_specs=[pl.BlockSpec(memory_space=pltpu.HBM if at < kept else pltpu.VMEM) for at in range(len(outs))],
            scratch_shapes=scratch,
            compiler_params=pltpu.CompilerParams(vmem_limit_bytes=vmem * MIB),
            cost_estimate=pl.CostEstimate(flops=flops, bytes_accessed=8 * 2**20, transcendentals=2**19),
            name=name,
        )(*args)

    return run


def swapped(block, axis, size, bit):
    return lax.ppermute(block, axis, [(i, i ^ bit) for i in range(size)])


def body(tokens, cotangent, region, gain, w_qkv, w_proj):
    x = tokens.transpose(1, 0, 2)
    g = cotangent.transpose(1, 0, 2)
    edges = [((rows, 2 * D), BF16) for rows in (LON_ROWS, LAT_ROWS, COR_ROWS)]
    where = jnp.stack([lax.axis_index("core"), (lax.axis_index(LAT_AXES) == 15).astype(jnp.int32)]).astype(jnp.int32)
    constant = functools.partial(jnp.asarray, dtype=BF16)
    picks = [inner_pick(), edge_pick(0), edge_pick(1), last_pick()]
    weights = [((D, 3 * D), BF16), ((D, D), BF16)]
    slab = ((2 * WIN_LAT, ROWS_LON, D), BF16)
    loaded = [slab, slab] + weights + [(pick.shape, BF16) for pick in picks]
    loaded += [((2, 2 * WIN_LAT, 16, D), BF16), ((2, SHIFT_LAT, ROWS_LON, D), BF16), ((COLS_LAT, ROWS_LON), jnp.int32)]
    scratch = [pltpu.VMEM((2, COLS_LAT, 2 * EDGE, D), BF16), pltpu.VMEM((2, SHIFT_LAT, ROWS_LON, D), BF16)]
    scratch += [pltpu.SemaphoreType.DMA((17,))]
    e_lon, e_lat, e_cor, x_s, g_s, wqkv_s, wproj_s, pick, pick0, pick1, pick2, ends, tails, ids = call(
        edges_kernel, edges + loaded, scratch, 10**6, "edges", 1, far=9, vmem=12
    )(where, x, g, region.T, w_qkv, w_proj, *[constant(pick) for pick in picks])
    lon_back = [((i + 1) % 16, i) for i in range(16)]
    lat_back = lon_back
    both_back = [(((i + 1) % 16) * 16 + (j + 1) % 16, i * 16 + j) for i in range(16) for j in range(16)]
    h_lon = lax.ppermute(e_lon, LON_AXES, lon_back)
    h_lat = lax.ppermute(e_lat, LAT_AXES, lat_back)
    h_cor = lax.ppermute(e_cor, LON_AXES + LAT_AXES, both_back)

    gain_row = gain.reshape(1, D)
    acts = [((HALF, D), BF16), ((HALF, D), BF16), ((HALF, D), BF16), ((HALF, 3 * D), BF16)]
    x1, g1, att1, dp1, gqkv1, gproj1 = call(
        first_kernel, acts + [((D, 3 * D), F32), ((D, D), F32)], pass_scratch(), 4 * 10**9, "inner", kept=4
    )(x_s, g_s, wqkv_s, wproj_s, pick, ids, gain_row)

    width = 2 * D + 128
    x2, g2, att2, dp2, keep, send = call(
        second_kernel,
        acts + [((16 * PIECES, width), BF16)] * 2,
        pass_scratch() + [pltpu.VMEM((D, 4 * D), F32)],
        4 * 10**9,
        "outer",
        1,
        kept=4,
    )(
        where, h_lon, h_lat, h_cor, gain_row, gqkv1, gproj1, wqkv_s, wproj_s, pick0, pick1, pick2, ends, tails, ids
    )

    scratch = [pltpu.VMEM((16 * PIECES, width), BF16), pltpu.SemaphoreType.DMA((8,))]
    (mine,) = call(add_out_kernel, [((16 * PIECES, width), BF16)], scratch, 10**5, "add", kept=1, vmem=8)(
        keep, swapped(send, "core", 2, 1)
    )
    mine, x1, x2 = lax.optimization_barrier((mine, x1, x2))
    pieces = lax.all_to_all(mine.reshape(PIECES, 16, -1), PLANE, 0, 0, tiled=True)
    mixed_c, tgrad_c, s_lon, s_lat, s_cor = call(
        third_kernel,
        [((COLS_LAT, ROWS_LON, D), BF16)] * 2
        + edges,
        [pltpu.VMEM((2 * HALF, D), F32)] * 2
        + [pltpu.VMEM((2, HALF, D), BF16)] * 3
        + [pltpu.VMEM((2, HALF, 3 * D), BF16), pltpu.VMEM((SLAB, 4 * WIN), BF16)]
        + [pltpu.VMEM(*weight) for weight in weights]
        + [pltpu.SemaphoreType.DMA((11,))],
        4 * 10**9,
        "tokens",
        far=11,
        vmem=28,
    )(x1, g1, att1, dp1, x2, g2, att2, dp2, constant(slab_place()), w_qkv, w_proj, gain_row)
    lon_on = [(j, i) for i, j in lon_back]
    both_on = [(j, i) for i, j in both_back]
    t_lon = lax.ppermute(s_lon, LON_AXES, lon_on)
    t_lat = lax.ppermute(s_lat, LAT_AXES, lon_on)
    t_cor = lax.ppermute(s_cor, LON_AXES + LAT_AXES, both_on)

    (piece,) = call(sum_kernel, [((16, width), BF16)], [], 10**5, "sum", vmem=8)(pieces)
    (piece,) = call(add_kernel, [((16, width), BF16)], [], 10**5, "add", vmem=4)(piece, swapped(piece, "z_hi", 4, 1))
    received = swapped(piece, "z_hi", 4, 3)
    received, t_lon, t_lat, t_cor = lax.optimization_barrier((received, t_lon, t_lat, t_cor))
    copies, gain_tile = call(
        spread_kernel,
        [((PIECES, 16, 2 * D), BF16), ((16, 128), F32)],
        [pltpu.VMEM((16, 2 * D), BF16), pltpu.SemaphoreType.DMA((PIECES,))],
        10**5,
        "spread",
        kept=1,
        vmem=4,
    )(piece, received)
    gain_grad = gain_tile[:4].reshape(D) / gain
    grads = lax.all_to_all(copies, PLANE, 0, 0, tiled=True)
    mixed, tokens_grad = call(restore_kernel, [((COLS_LAT, ROWS_LON, D), BF16)] * 2, [], 10**6, "restore", vmem=10)(
        mixed_c, tgrad_c, t_lon, t_lat, t_cor
    )
    grads, mixed, tokens_grad = lax.optimization_barrier((grads, mixed, tokens_grad))
    grads = grads.reshape(16 * PIECES, 2 * D)
    other = swapped(grads, "core", 2, 1)
    core = where[:1]
    qkv_grad, proj_grad = place(1 - core, other, *place(core, grads))

    return mixed.transpose(1, 0, 2), tokens_grad.transpose(1, 0, 2), qkv_grad, proj_grad, gain_grad


def solution(mesh):
    fine = Mesh(mesh.devices.reshape(2, 4, 2, 2, 4, 2), ("y_lo", "z_hi", "z_lo", "y_hi", "x", "core"))
    grid = P(LON_AXES, LAT_AXES, None)
    return jax.shard_map(
        body,
        mesh=fine,
        in_specs=(grid, grid, P(LON_AXES, LAT_AXES), P(), P(), P()),
        out_specs=(grid, grid, P(), P(), P()),
        check_vma=False,
    )
```

```python
import functools

import jax
import jax.numpy as jnp
import numpy as np
from jax import lax
from jax.experimental import pallas as pl
from jax.experimental.pallas import tpu as pltpu
from jax.sharding import Mesh, PartitionSpec as P

HEADS = 8
HEAD_DIM = 64
WIN_LON = 12
WIN_LAT = 6
WIN = WIN_LON * WIN_LAT
SHIFT_LON = 6
SHIFT_LAT = 3
D = 512
ROWS_LON = 48
COLS_LAT = 18
SLAB = WIN_LAT * ROWS_LON
EDGE = 8
HALF = 6 * WIN
PIECES = 32
LON_ROWS, LAT_ROWS, COR_ROWS = 96, 128, 32
LON_IDS, LAT_IDS, COR_IDS = 90, 126, 18
F32 = jnp.float32
BF16 = jnp.bfloat16
MIB = 1024 * 1024

PLANE = ("y_lo", "z_lo", "y_hi", "x")
LON_AXES = ("y_lo", "z_hi", "z_lo")
LAT_AXES = ("y_hi", "x", "core")


def window_source(window, row):
    jj, ii = divmod(row, WIN_LON)
    return jj, (window * WIN_LON + ii + SHIFT_LON) % ROWS_LON


def inner_pick():
    out = np.zeros((3 * WIN, SLAB), np.float32)
    for window in range(3):
        for row in range(WIN):
            jj, i = window_source(window, row)
            out[window * WIN + row, jj * ROWS_LON + i] = 1
    return out


def edge_pick(column):
    out = np.zeros((WIN, WIN_LAT * 16 + LON_ROWS), np.float32)
    for row in range(WIN):
        jj, i = window_source(3, row)
        if i >= SHIFT_LON:
            out[row, jj * 16 + i - 32] = 1
        else:
            out[row, WIN_LAT * 16 + (column * WIN_LAT + jj) * SHIFT_LON + i] = 1
    return out


def last_pick():
    own = SHIFT_LAT * ROWS_LON
    out = np.zeros((4 * WIN, own + LAT_ROWS + LON_ROWS + COR_ROWS), np.float32)
    for window in range(4):
        for row in range(WIN):
            jj, i = window_source(window, row)
            if i >= SHIFT_LON and jj < SHIFT_LAT:
                at = jj * ROWS_LON + i
            elif i >= SHIFT_LON:
                at = own + (jj - SHIFT_LAT) * (ROWS_LON - SHIFT_LON) + i - SHIFT_LON
            elif jj < SHIFT_LAT:
                at = own + LAT_ROWS + (2 * WIN_LAT + jj) * SHIFT_LON + i
            else:
                at = own + LAT_ROWS + LON_ROWS + (jj - SHIFT_LAT) * SHIFT_LON + i
            out[window * WIN + row, at] = 1
    return out


def slab_place():
    out = np.zeros((SLAB, 4 * WIN), np.float32)
    for window in range(4):
        for row in range(WIN):
            jj, i = window_source(window, row)
            out[jj * ROWS_LON + i, window * WIN + row] = 1
    return out


def dot(a, b):
    return jnp.dot(a, b, preferred_element_type=F32)


def dot_nt(a, b):
    return lax.dot_general(a, b, (((1,), (1,)), ((), ())), preferred_element_type=F32)


def dot_tn(a, b):
    return lax.dot_general(a, b, (((0,), (0,)), ((), ())), preferred_element_type=F32)


def normalise(x):
    centred = x - jnp.mean(x, axis=-1, keepdims=True)
    variance = jnp.mean(centred * centred, axis=-1, keepdims=True)
    inverse = lax.rsqrt(variance + 1e-05)
    return centred * inverse, inverse


def staged(pairs, sems):
    copies = [pltpu.make_async_copy(source, scratch, sems.at[at]) for at, (source, scratch) in enumerate(pairs)]
    for copy in copies:
        copy.start()
    return copies


def rows_of(shape, where):
    row = lax.broadcasted_iota(jnp.int32, shape, 0)
    return jnp.where(lax.broadcasted_iota(jnp.int32, shape, 1) == where(row), 1.0, 0.0).astype(BF16)


def strip_row(first, pitch):
    def where(row):
        lat = (row * 10923) >> 16
        return (lat + first) * pitch + row - lat * SHIFT_LON

    return where


def slab_row(row):
    lat = (row >= 42).astype(jnp.int32) + (row >= 84).astype(jnp.int32)
    return jnp.where(row < LAT_IDS, lat * ROWS_LON + SHIFT_LON + row - lat * 42, -1)


def spread_row(kept):
    def where(row):
        lat, lon = row >> 3, row & 7
        return jnp.where((lon < SHIFT_LON) & (lat < kept), lat * SHIFT_LON + lon, -1)

    return where


def wide_row(row):
    lat = (row >= 48).astype(jnp.int32) + (row >= 96).astype(jnp.int32)
    lon = row - lat * ROWS_LON
    return jnp.where(lon >= SHIFT_LON, lat * 42 + lon - SHIFT_LON, -1)


def diagonal(rows):
    shape = (rows, 128)
    return lax.broadcasted_iota(jnp.int32, shape, 0) == lax.broadcasted_iota(jnp.int32, shape, 1)


def region_marks(region, lats):
    columns = region.T
    return jnp.concatenate(
        [jnp.broadcast_to(columns[:, lat : lat + 1], (ROWS_LON, 128)) for lat in lats], 0
    ).astype(BF16)


def windows_pass(
    x_w, g_w, lab_w, gain, wqkv, wproj, att_o, dp_o, att_b, dp_b, stores, out_sems, proj, gatt, onehot, att, dp
):
    normed, _ = normalise(x_w[...].astype(F32))
    hidden = (normed * gain[...]).astype(BF16)
    proj[...] = dot(hidden, wqkv[...])
    gatt[...] = dot_nt(g_w[...], wproj[...])
    lane = lax.broadcasted_iota(jnp.int32, (HALF, 128), 1).astype(F32)
    onehot[...] = jnp.where(lab_w == lane, 1.0, 0.0)
    low = lax.broadcasted_iota(jnp.int32, (WIN, 128), 1) < HEAD_DIM

    def stacked(pair):
        return jnp.concatenate([jnp.where(low, pair, 0.0), jnp.where(low, 0.0, pair)], 0)

    def unstacked(both):
        return jnp.where(low, both[:WIN], both[WIN:])

    def one_window(window):
        rows = pl.ds(window * WIN, WIN)
        marks = onehot[rows, :]
        marks_q = jnp.concatenate([marks, marks], 0).astype(BF16)
        bar_k = ((marks - 1.0) * 1e30).astype(BF16)
        pairs = range(HEADS // 2)
        q, k, v, do = [], [], [], []
        for pair in pairs:
            cols = pl.ds(pair * 128, 128)
            q.append(stacked(proj[rows, pl.ds(pair * 128, 128)].astype(BF16).astype(F32) * HEAD_DIM**-0.5).astype(BF16))
            k.append(proj[rows, pl.ds(D + pair * 128, 128)].astype(BF16))
            v.append(proj[rows, pl.ds(2 * D + pair * 128, 128)].astype(BF16))
            do.append(stacked(gatt[rows, cols]).astype(BF16))
        s = [dot_nt(jnp.concatenate([k[p], bar_k], 1), jnp.concatenate([q[p], marks_q], 1)) for p in pairs]
        da = [dot_nt(v[p], do[p]) for p in pairs]
        a, ab, ds = [], [], []
        for p in pairs:
            lifted = jnp.exp(s[p] - jnp.max(s[p], axis=0, keepdims=True))
            a.append(lifted * (1.0 / jnp.sum(lifted, axis=0, keepdims=True)))
            ab.append(a[p].astype(BF16))
        for p in pairs:
            inner = jnp.sum(da[p] * a[p], axis=0, keepdims=True)
            ds.append((a[p] * (da[p] - inner)).astype(BF16))
        for p in pairs:
            cols = pl.ds(p * 128, 128)
            att[rows, cols] = unstacked(dot_tn(ab[p], v[p]))
            dp[rows, pl.ds(2 * D + p * 128, 128)] = dot(ab[p], do[p])
            dp[rows, cols] = unstacked(dot_tn(ds[p], k[p])) * HEAD_DIM**-0.5
            dp[rows, pl.ds(D + p * 128, 128)] = dot(ds[p], q[p])

    for window in range(6):
        one_window(window)
        if window % 2:
            rows = pl.ds((window - 1) * WIN, 2 * WIN)
            att_b[rows, :] = att[rows, :].astype(BF16)
            dp_b[rows, :] = dp[rows, :].astype(BF16)
            pairs = [(att_b.at[rows], att_o.at[rows]), (dp_b.at[rows], dp_o.at[rows])]
            stores.extend(staged(pairs, out_sems.at[1 + window // 2]))
    return hidden


def first_kernel(
    x, g, wqkv, wproj, pick, region, gain, x_o, g_o, att_o, dp_o, gqkv, gproj,
    proj, gatt, onehot, att, dp, x_w, g_w, att_b, dp_b, out_sems,
):
    ids = region[...].astype(F32)
    parts = {"r": []}
    for column in range(2):
        start = SHIFT_LAT + column * WIN_LAT
        parts["r"].append(dot(pick[...], region_marks(ids, range(start, start + WIN_LAT))))
    parts["r"] = jnp.concatenate(parts["r"], 0)
    for name, ref in (("x", x), ("g", g)):
        got = []
        for column in range(2):
            start = column * WIN_LAT
            got.append(dot(pick[...], ref[start : start + WIN_LAT].reshape(SLAB, D)))
        parts[name] = jnp.concatenate(got, 0)
    x_w[...] = parts["x"].astype(BF16)
    g_w[...] = parts["g"].astype(BF16)
    stores = staged([(x_w, x_o), (g_w, g_o)], out_sems.at[0])
    hidden = windows_pass(
        x_w, g_w, parts["r"], gain, wqkv, wproj, att_o, dp_o, att_b, dp_b, stores, out_sems, proj, gatt, onehot, att, dp
    )
    gqkv[...] = dot_tn(hidden, dp_b[...])
    gproj[...] = dot_tn(att_b[...], g_w[...])
    for store in stores:
        store.wait()


def second_kernel(
    where, h_lon, h_lat, h_cor, gain, gqkv1, gproj1, wqkv, wproj, pick0, pick1, pick2, ends, tails, region,
    x_o, g_o, att_o, dp_o, keep, send, proj, gatt, onehot, att, dp, x_w, g_w, att_b, dp_b, out_sems, total,
):
    parts = []
    ids = region[...].astype(F32)
    halos = ((h_lon, LON_ROWS, LON_IDS), (h_lat, LAT_ROWS, LAT_IDS), (h_cor, COR_ROWS, COR_IDS))
    for array in range(3):
        if array == 2:
            halo = []
            for packed, rows, at in halos:
                line = packed[pl.ds(at // 16 * 16, 16), pl.ds(0, 128)].astype(F32)[at % 16 : at % 16 + 1]
                column = jnp.sum(jnp.where(diagonal(rows), line, 0.0), axis=1, keepdims=True)
                halo.append(jnp.broadcast_to(column, (rows, 128)).astype(BF16))
        else:
            halo = [packed[:, pl.ds(array * D, D)] for packed, _, _ in halos]

        got = []
        for column, pick in ((0, pick0), (1, pick1)):
            first = column * WIN_LAT
            if array == 2:
                marks = region_marks(ids, range(SHIFT_LAT + first, SHIFT_LAT + first + WIN_LAT))
                own = jnp.concatenate([marks[lat * ROWS_LON + 32 : (lat + 1) * ROWS_LON] for lat in range(WIN_LAT)], 0)
            else:
                own = ends[array, first : first + WIN_LAT].reshape(WIN_LAT * 16, D)
            got.append(dot(pick[...], jnp.concatenate([own, halo[0]], 0)))
        if array == 2:
            own = region_marks(ids, range(COLS_LAT - SHIFT_LAT, COLS_LAT))
        else:
            own = tails[array].reshape(SHIFT_LAT * ROWS_LON, D)
        got.append(dot(pick2[...], jnp.concatenate([own, halo[1], halo[0], halo[2]], 0)))
        parts.append(jnp.concatenate(got, 0))
    x_w[...] = parts[0].astype(BF16)
    g_w[...] = parts[1].astype(BF16)
    stores = staged([(x_w, x_o), (g_w, g_o)], out_sems.at[0])
    row = lax.broadcasted_iota(jnp.int32, (HALF, 128), 0)
    past = jnp.zeros((HALF, 128), jnp.bool_)
    for window in range(2, 6):
        past = past | ((row >= window * WIN + WIN // 2) & (row < (window + 1) * WIN))
    labels = parts[2] + jnp.where(past, 3.0, 0.0) * where[1].astype(F32)
    hidden = windows_pass(
        x_w, g_w, labels, gain, wqkv, wproj, att_o, dp_o, att_b, dp_b, stores, out_sems, proj, gatt, onehot, att, dp
    )
    total[:, pl.ds(0, 3 * D)] = gqkv1[...] + dot_tn(hidden, dp_b[...])
    total[:, pl.ds(3 * D, D)] = gproj1[...] + dot_tn(att_b[...], g_w[...])
    scaled = jnp.sum(total[:, pl.ds(0, 3 * D)] * wqkv[...].astype(F32), axis=1, keepdims=True)
    line = [
        jnp.sum(jnp.where(diagonal(128), scaled[at * 128 : (at + 1) * 128], 0.0), axis=0, keepdims=True) for at in range(4)
    ]
    tile = jnp.concatenate(line + [jnp.zeros((12, 128), F32)], 0).astype(BF16)
    core = where[0]
    for ref, half in ((keep, core), (send, 1 - core)):
        rows = pl.ds(pl.multiple_of(half * 256, 256), 256)
        for side in range(2):
            ref[pl.ds(side * 256, 256), pl.ds(0, 2 * D)] = total[rows, pl.ds(side * 2 * D, 2 * D)].astype(BF16)
        for piece in range(PIECES):
            ref[pl.ds(piece * 16, 16), pl.ds(2 * D, 128)] = tile
    for store in stores:
        store.wait()


def third_kernel(
    x1_h, g1_h, att1_h, dp1_h, x2_h, g2_h, att2_h, dp2_h, place_h, wqkv_h, wproj_h, gain,
    mixed, tgrad, s_lon, s_lat, s_cor, mixed_f, tgrad_f, xs, gs, atts, dps, place, wqkv, wproj, sems,
):
    first = [(wproj_h, wproj), (wqkv_h, wqkv), (x1_h, xs.at[0]), (att1_h, atts.at[0]), (dp1_h, dps.at[0])]
    second = [(g1_h, gs.at[0]), (x2_h, xs.at[1]), (att2_h, atts.at[1]), (dp2_h, dps.at[1]), (g2_h, gs.at[1])]
    loads = staged(first + second + [(place_h, place)], sems)
    for at in range(2):
        for load in loads[:6] if at == 0 else loads[6:]:
            load.wait()
        x, g, att, dp = xs.at[at], gs.at[at], atts.at[at], dps.at[at]
        rows = pl.ds(at * HALF, HALF)
        flat = x[...].astype(F32)
        mixed_f[rows, :] = flat + dot(att[...], wproj[...])
        normed, inverse = normalise(flat)
        grad_normed = dot_nt(dp[...], wqkv[...]) * gain[...]
        grad_input = inverse * (
            grad_normed
            - jnp.mean(grad_normed, axis=-1, keepdims=True)
            - normed * jnp.mean(grad_normed * normed, axis=-1, keepdims=True)
        )
        tgrad_f[rows, :] = g[...].astype(F32) + grad_input
    for at, (ref, out) in enumerate(((mixed_f, mixed), (tgrad_f, tgrad))):
        lanes = pl.ds(at * D, D)
        strips = []
        for column in range(3):
            if column < 2:
                ordered = jnp.concatenate(
                    [ref[pl.ds(column * 3 * WIN, 3 * WIN), :], ref[pl.ds(HALF + column * WIN, WIN), :]], 0
                )
            else:
                ordered = ref[pl.ds(HALF + 2 * WIN, 4 * WIN), :]
            slab = dot(place[...], ordered.astype(BF16)).reshape(WIN_LAT, ROWS_LON, D)
            out[column * WIN_LAT : (column + 1) * WIN_LAT] = slab.astype(BF16)
            strips.append(slab[:, :EDGE].reshape(WIN_LAT * EDGE, D))
        strip = jnp.concatenate(strips, 0).astype(BF16)
        last = slab[SHIFT_LAT:].reshape(SHIFT_LAT * ROWS_LON, D).astype(BF16)
        s_lon[:, lanes] = dot(rows_of((LON_ROWS, COLS_LAT * EDGE), strip_row(0, EDGE)), strip).astype(BF16)
        s_lat[:, lanes] = dot(rows_of((LAT_ROWS, SHIFT_LAT * ROWS_LON), slab_row), last).astype(BF16)
        s_cor[:, lanes] = dot(rows_of((COR_ROWS, COLS_LAT * EDGE), strip_row(15, EDGE)), strip).astype(BF16)


def restore_kernel(mixed_c, tgrad_c, h_lon, h_lat, h_cor, mixed, tgrad):
    kept = COLS_LAT - SHIFT_LAT
    first = lax.broadcasted_iota(jnp.int32, (EDGE, D), 0) < SHIFT_LON
    for at, (own, out) in enumerate(((mixed_c, mixed), (tgrad_c, tgrad))):
        lanes = pl.ds(at * D, D)
        out[SHIFT_LAT:] = own[:kept]
        lon = dot(rows_of((kept * EDGE, LON_ROWS), spread_row(kept)), h_lon[:, lanes])
        cor = dot(rows_of((SHIFT_LAT * EDGE, COR_ROWS), spread_row(SHIFT_LAT)), h_cor[:, lanes])
        lat = dot(rows_of((SHIFT_LAT * ROWS_LON, LAT_ROWS), wide_row), h_lat[:, lanes])
        for row in range(COLS_LAT):
            if row < SHIFT_LAT:
                strip = cor[row * EDGE : (row + 1) * EDGE]
                inner = lat[row * ROWS_LON : (row + 1) * ROWS_LON]
                whole = jnp.concatenate([jnp.where(first, strip, inner[:EDGE]), inner[EDGE:]], 0)
                out[row] = whole.astype(BF16)
            else:
                strip = lon[(row - SHIFT_LAT) * EDGE : (row - SHIFT_LAT + 1) * EDGE]
                inner = own[row - SHIFT_LAT, pl.ds(0, 2 * EDGE), :].astype(F32)
                whole = jnp.concatenate([jnp.where(first, strip, inner[:EDGE]), inner[EDGE:]], 0)
                out[row, pl.ds(0, 2 * EDGE), :] = whole.astype(BF16)


def add_out_kernel(keep, received, out, total, sems):
    copies = []
    for part in range(8):
        rows = pl.ds(part * 64, 64)
        total[rows, :] = (keep[rows, :].astype(F32) + received[rows, :].astype(F32)).astype(BF16)
        copies.append(pltpu.make_async_copy(total.at[rows], out.at[rows], sems.at[part]))
        copies[-1].start()
    for copy in copies:
        copy.wait()


def sum_kernel(pieces, out):
    total = pieces[0].astype(F32)
    for piece in range(1, PIECES):
        total = total + pieces[piece].astype(F32)
    out[...] = total.astype(BF16)


def spread_kernel(piece, second, first, third, copies, gain, total, sems):
    both = piece[...].astype(F32) + first[...].astype(F32)
    both = both + (second[...].astype(F32) + third[...].astype(F32))
    total[...] = both[:, : 2 * D].astype(BF16)
    sent = staged([(total, copies.at[at]) for at in range(PIECES)], sems)
    gain[...] = both[:, 2 * D :].astype(BF16).astype(F32)
    for copy in sent:
        copy.wait()


def place_kernel(later, half, grads, *refs):
    gqkv, gproj, wide, square, sems = refs[2:] if later else refs
    copies = []
    for part in range(4):
        rows = pl.ds(part * 64, 64)
        right = pl.ds(256 + part * 64, 64)
        wide[rows, pl.ds(0, 2 * D)] = grads[rows, :].astype(F32)
        wide[rows, pl.ds(2 * D, D)] = grads[right, pl.ds(0, D)].astype(F32)
        square[rows, :] = grads[right, pl.ds(D, D)].astype(F32)
        there = pl.ds(pl.multiple_of(half[0] * 256 + part * 64, 64), 64)
        for at, (source, out) in enumerate(((wide, gqkv), (square, gproj))):
            copies.append(pltpu.make_async_copy(source.at[rows], out.at[there], sems.at[part, at]))
            copies[-1].start()
    for copy in copies:
        copy.wait()


def place(half, grads, *filled):
    hbm = pl.BlockSpec(memory_space=pl.ANY)
    return pl.pallas_call(
        functools.partial(place_kernel, bool(filled)),
        out_shape=[jax.ShapeDtypeStruct((D, 3 * D), F32), jax.ShapeDtypeStruct((D, D), F32)],
        in_specs=[pl.BlockSpec(memory_space=pltpu.SMEM), pl.BlockSpec(memory_space=pltpu.VMEM)] + [hbm] * len(filled),
        out_specs=[hbm, hbm],
        input_output_aliases={2: 0, 3: 1} if filled else {},
        scratch_shapes=[
            pltpu.VMEM((256, 3 * D), F32),
            pltpu.VMEM((256, D), F32),
            pltpu.SemaphoreType.DMA((4, 2)),
        ],
        compiler_params=pltpu.CompilerParams(vmem_limit_bytes=8 * MIB),
        cost_estimate=pl.CostEstimate(flops=10**6, bytes_accessed=3 * 2**20, transcendentals=0),
        name="place",
    )(half, grads, *filled)


def edges_kernel(
    where, x_h, g_h, region_h, wqkv_h, wproj_h, pick_h, pick0_h, pick1_h, pick2_h,
    h_lon, h_lat, h_cor, x, g, wqkv, wproj, pick, pick0, pick1, pick2, ends, tails, region, strips, slabs, sems,
):
    lats = pl.ds(SHIFT_LAT, 2 * WIN_LAT)
    end = pl.ds(COLS_LAT - SHIFT_LAT, SHIFT_LAT)
    loads = [(region_h, region)]
    for at, ref in enumerate((x_h, g_h)):
        loads += [(ref.at[:, pl.ds(0, 2 * EDGE), :], strips.at[at]), (ref.at[pl.ds(0, SHIFT_LAT)], slabs.at[at])]
    loads += [(pick_h, pick), (x_h.at[lats], x), (g_h.at[lats], g), (wqkv_h, wqkv), (wproj_h, wproj)]
    loads += [(pick0_h, pick0), (pick1_h, pick1), (pick2_h, pick2)]
    for at, ref in enumerate((x_h, g_h)):
        loads += [(ref.at[lats, pl.ds(32, 16), :], ends.at[at]), (ref.at[end], tails.at[at])]
    loads = staged(loads, sems)
    for load in loads[:5]:
        load.wait()
    ids = region[...].astype(F32)
    marks = region_marks(ids, range(COLS_LAT))
    strip = jnp.concatenate([marks[lat * ROWS_LON : lat * ROWS_LON + 2 * EDGE] for lat in range(COLS_LAT)], 0)
    width = COLS_LAT * 2 * EDGE
    slab = SHIFT_LAT * ROWS_LON
    for out, rows, at, chosen, source in (
        (h_lon, LON_ROWS, LON_IDS, rows_of((LON_ROWS, width), strip_row(SHIFT_LAT, 2 * EDGE)), strip),
        (h_lat, LAT_ROWS, LAT_IDS, rows_of((LAT_ROWS, slab), slab_row), marks[:slab]),
        (h_cor, COR_ROWS, COR_IDS, rows_of((COR_ROWS, width), strip_row(0, 2 * EDGE)), strip),
    ):
        line = jnp.sum(jnp.where(diagonal(rows), dot(chosen, source), 0.0), axis=0, keepdims=True)
        line = jnp.concatenate([line] * (D // 128), 1)
        here = lax.broadcasted_iota(jnp.int32, (rows, D), 0) == at
        for array in range(2):
            tokens = slabs[array].reshape(slab, D) if out is h_lat else strips[array].reshape(width, D)
            out[:, pl.ds(array * D, D)] = jnp.where(here, line, dot(chosen, tokens)).astype(BF16)
    for load in loads[5:]:
        load.wait()


def pass_scratch():
    return [
        pltpu.VMEM((HALF, 3 * D), F32),
        pltpu.VMEM((HALF, D), F32),
        pltpu.VMEM((HALF, 128), F32),
        pltpu.VMEM((HALF, D), F32),
        pltpu.VMEM((HALF, 3 * D), F32),
        pltpu.VMEM((HALF, D), BF16),
        pltpu.VMEM((HALF, D), BF16),
        pltpu.VMEM((HALF, D), BF16),
        pltpu.VMEM((HALF, 3 * D), BF16),
        pltpu.SemaphoreType.DMA((4, 2)),
    ]


def call(kernel, outs, scratch, flops, name, scalars=0, far=0, kept=0, vmem=24):
    def run(*args):
        args = list(args)
        for at in range(scalars, scalars + far):
            args[at] = pltpu.with_memory_space_constraint(args[at], pltpu.HBM)
        specs = [pl.BlockSpec(memory_space=pltpu.SMEM)] * scalars
        specs += [pl.BlockSpec(memory_space=pltpu.HBM)] * far
        specs += [pl.BlockSpec(memory_space=pltpu.VMEM)] * (len(args) - scalars - far)
        return pl.pallas_call(
            kernel,
            out_shape=[pltpu.HBM(*out) if at < kept else jax.ShapeDtypeStruct(*out) for at, out in enumerate(outs)],
            in_specs=specs,
            out_specs=[pl.BlockSpec(memory_space=pltpu.HBM if at < kept else pltpu.VMEM) for at in range(len(outs))],
            scratch_shapes=scratch,
            compiler_params=pltpu.CompilerParams(vmem_limit_bytes=vmem * MIB),
            cost_estimate=pl.CostEstimate(flops=flops, bytes_accessed=8 * 2**20, transcendentals=2**19),
            name=name,
        )(*args)

    return run


def swapped(block, axis, size, bit):
    return lax.ppermute(block, axis, [(i, i ^ bit) for i in range(size)])


def body(tokens, cotangent, region, gain, w_qkv, w_proj):
    x = tokens.transpose(1, 0, 2)
    g = cotangent.transpose(1, 0, 2)
    edges = [((rows, 2 * D), BF16) for rows in (LON_ROWS, LAT_ROWS, COR_ROWS)]
    where = jnp.stack([lax.axis_index("core"), (lax.axis_index(LAT_AXES) == 15).astype(jnp.int32)]).astype(jnp.int32)
    constant = functools.partial(jnp.asarray, dtype=BF16)
    picks = [inner_pick(), edge_pick(0), edge_pick(1), last_pick()]
    weights = [((D, 3 * D), BF16), ((D, D), BF16)]
    slab = ((2 * WIN_LAT, ROWS_LON, D), BF16)
    loaded = [slab, slab] + weights + [(pick.shape, BF16) for pick in picks]
    loaded += [((2, 2 * WIN_LAT, 16, D), BF16), ((2, SHIFT_LAT, ROWS_LON, D), BF16), ((COLS_LAT, ROWS_LON), jnp.int32)]
    scratch = [pltpu.VMEM((2, COLS_LAT, 2 * EDGE, D), BF16), pltpu.VMEM((2, SHIFT_LAT, ROWS_LON, D), BF16)]
    scratch += [pltpu.SemaphoreType.DMA((17,))]
    e_lon, e_lat, e_cor, x_s, g_s, wqkv_s, wproj_s, pick, pick0, pick1, pick2, ends, tails, ids = call(
        edges_kernel, edges + loaded, scratch, 10**6, "edges", 1, far=9, vmem=12
    )(where, x, g, region.T, w_qkv, w_proj, *[constant(pick) for pick in picks])
    lon_back = [((i + 1) % 16, i) for i in range(16)]
    lat_back = lon_back
    both_back = [(((i + 1) % 16) * 16 + (j + 1) % 16, i * 16 + j) for i in range(16) for j in range(16)]
    h_lon = lax.ppermute(e_lon, LON_AXES, lon_back)
    h_lat = lax.ppermute(e_lat, LAT_AXES, lat_back)
    h_cor = lax.ppermute(e_cor, LON_AXES + LAT_AXES, both_back)

    gain_row = gain.reshape(1, D)
    acts = [((HALF, D), BF16), ((HALF, D), BF16), ((HALF, D), BF16), ((HALF, 3 * D), BF16)]
    x1, g1, att1, dp1, gqkv1, gproj1 = call(
        first_kernel, acts + [((D, 3 * D), F32), ((D, D), F32)], pass_scratch(), 4 * 10**9, "inner", kept=4
    )(x_s, g_s, wqkv_s, wproj_s, pick, ids, gain_row)

    width = 2 * D + 128
    x2, g2, att2, dp2, keep, send = call(
        second_kernel,
        acts + [((16 * PIECES, width), BF16)] * 2,
        pass_scratch() + [pltpu.VMEM((D, 4 * D), F32)],
        4 * 10**9,
        "outer",
        1,
        kept=4,
    )(
        where, h_lon, h_lat, h_cor, gain_row, gqkv1, gproj1, wqkv_s, wproj_s, pick0, pick1, pick2, ends, tails, ids
    )

    scratch = [pltpu.VMEM((16 * PIECES, width), BF16), pltpu.SemaphoreType.DMA((8,))]
    (mine,) = call(add_out_kernel, [((16 * PIECES, width), BF16)], scratch, 10**5, "add", kept=1, vmem=8)(
        keep, swapped(send, "core", 2, 1)
    )
    mine, x1, x2 = lax.optimization_barrier((mine, x1, x2))
    pieces = lax.all_to_all(mine.reshape(PIECES, 16, -1), PLANE, 0, 0, tiled=True)
    mixed_c, tgrad_c, s_lon, s_lat, s_cor = call(
        third_kernel,
        [((COLS_LAT, ROWS_LON, D), BF16)] * 2
        + edges,
        [pltpu.VMEM((2 * HALF, D), F32)] * 2
        + [pltpu.VMEM((2, HALF, D), BF16)] * 3
        + [pltpu.VMEM((2, HALF, 3 * D), BF16), pltpu.VMEM((SLAB, 4 * WIN), BF16)]
        + [pltpu.VMEM(*weight) for weight in weights]
        + [pltpu.SemaphoreType.DMA((11,))],
        4 * 10**9,
        "tokens",
        far=11,
        vmem=28,
    )(x1, g1, att1, dp1, x2, g2, att2, dp2, constant(slab_place()), w_qkv, w_proj, gain_row)
    lon_on = [(j, i) for i, j in lon_back]
    both_on = [(j, i) for i, j in both_back]
    t_lon = lax.ppermute(s_lon, LON_AXES, lon_on)
    t_lat = lax.ppermute(s_lat, LAT_AXES, lon_on)
    t_cor = lax.ppermute(s_cor, LON_AXES + LAT_AXES, both_on)

    (piece,) = call(sum_kernel, [((16, width), BF16)], [], 10**5, "sum", vmem=8)(pieces)
    received = [swapped(piece, "z_hi", 4, bit) for bit in (2, 1, 3)]
    received, t_lon, t_lat, t_cor = lax.optimization_barrier((received, t_lon, t_lat, t_cor))
    copies, gain_tile = call(
        spread_kernel,
        [((PIECES, 16, 2 * D), BF16), ((16, 128), F32)],
        [pltpu.VMEM((16, 2 * D), BF16), pltpu.SemaphoreType.DMA((PIECES,))],
        10**5,
        "spread",
        kept=1,
        vmem=4,
    )(piece, *received)
    gain_grad = gain_tile[:4].reshape(D) / gain
    grads = lax.all_to_all(copies, PLANE, 0, 0, tiled=True)
    mixed, tokens_grad = call(restore_kernel, [((COLS_LAT, ROWS_LON, D), BF16)] * 2, [], 10**6, "restore", vmem=10)(
        mixed_c, tgrad_c, t_lon, t_lat, t_cor
    )
    grads, mixed, tokens_grad = lax.optimization_barrier((grads, mixed, tokens_grad))
    grads = grads.reshape(16 * PIECES, 2 * D)
    other = swapped(grads, "core", 2, 1)
    core = where[:1]
    qkv_grad, proj_grad = place(1 - core, other, *place(core, grads))

    return mixed.transpose(1, 0, 2), tokens_grad.transpose(1, 0, 2), qkv_grad, proj_grad, gain_grad


def solution(mesh):
    fine = Mesh(mesh.devices.reshape(2, 4, 2, 2, 4, 2), ("y_lo", "z_hi", "z_lo", "y_hi", "x", "core"))
    grid = P(LON_AXES, LAT_AXES, None)
    return jax.shard_map(
        body,
        mesh=fine,
        in_specs=(grid, grid, P(LON_AXES, LAT_AXES), P(), P(), P()),
        out_specs=(grid, grid, P(), P(), P()),
        check_vma=False,
    )
```
